256 devices in a mesh: slab: 32 (over x, y, core), span: 8 (over z).
Axes of the slice: x: 4, y: 4, z: 8, core: 2. Of those that a mesh axis runs over, the one named last changes fastest.
Arguments:
- marker_force: float32 [3, 4194304], P(None, ('slab', 'span')), may hold values from -1.5 to 1.5
- marker_offset: float32 [3, 4194304], P(None, ('slab', 'span')), may hold values from 0 to 1
- marker_cell: int32 [3, 4194304], P(None, ('slab', 'span')), may hold values from 0 to 127, as said below
- marker_slab: int32 [4194304, 1], P(('slab', 'span')), may hold values from 0 to 31; in each aligned block of 16384 rows (0 to 16383, 16384 to 32767, ...) at most 1024 rows name the same one
Outputs:
- spectrum: float32 [2, 3, 64, 512, 128], P(None, None, 'slab', 'span')
The draws below stay inside these ranges and needn't reach their ends.
Inputs may be any that keep to these rules, and one draw needn't show every extreme that they name: `marker_slab`: among the 16384 markers of one device no slab index occurs more than 1024 times, and 1024 is reached. `marker_cell`: row 0 lies in 0 to 1, row 1 in 0 to 127, row 2 in 0 to 63.
All inputs are finite; a program needn't handle non-finite values.
Results may differ from the reference program's by a relative error of at most 0.0037.
Values sent between devices are 32-bit elements; how exact they have to be, the bound alone decides.
No kernel may reach another device: no remote copies, remote signals or barrier semaphores. Data moves between devices by JAX's collectives and lax.ppermute only.
A program may use at most 128 MiB of HBM per device.

```python
import math
import jax
import jax.numpy as jnp
import numpy as np
from jax import lax

CX = 2
NY = 128
NZ = 512
MK_DEV = 16384
SPAN_BLOCKS = 8
ZS = 64
NX = 64
CAP = 1024
MARKERS = 4194304
N_SLAB = 32


def draw_marker_cell(key, part):
    key = jax.random.fold_in(key, 11)
    bounds = jnp.array([CX, NY, ZS], dtype=jnp.int32)[:, None]
    return jax.random.randint(key, (3, MARKERS), 0, bounds, dtype=jnp.int32)


def shard_levels(own_key, shape, cuts, low, high):
    loudness = 1.0
    for dim, shards_of in cuts:
        draws = jax.random.uniform(jax.random.fold_in(jax.random.fold_in(own_key, 6), dim), (shards_of,), jnp.float32, low / len(cuts), high / len(cuts))
        loudness = loudness * jnp.repeat(jnp.exp(draws), shape[dim] // shards_of).reshape((-1,) + (1,) * (len(shape) - 1 - dim))
    return loudness


def deal_out(key, own, number, rows, count, top, most, slope):
    ranking = jax.random.permutation(key, count)
    crowded, common = portions_of(count, rows * top, most, slope, True), portions_of(count, rows * top, most, slope, False)
    places = jnp.arange(count)

    def named(tallies, offset_by):
        used = int((tallies > 0).sum())
        fixed = max(1, used // 4)
        shifted = fixed + (places - fixed + offset_by * (used - fixed)) % max(1, count - fixed)
        return jnp.zeros((count,), jnp.int32).at[ranking[jnp.where(places < fixed, places, shifted)]].set(jnp.asarray(tallies, jnp.int32))

    tallies = jnp.where(number % 4 == 0, named(crowded, number // 4), named(common, number - number // 4 - 1))
    mixed = jax.random.permutation(jax.random.fold_in(own, 3), count)
    donor, taker = mixed[0:count // 2 * 2:2], mixed[1:count // 2 * 2:2]
    margin = jnp.minimum(tallies[donor] - 1, most - tallies[taker]) // 2
    margin = jnp.where((donor == ranking[0]) | (taker == ranking[0]) | (tallies[taker] == 0), 0, jnp.maximum(margin, 0))
    shifted = jax.random.randint(jax.random.fold_in(own, 4), (count // 2,), 0, 1 << 20) % (margin + 1)
    tallies = tallies.at[donor].add(-shifted).at[taker].add(shifted)
    items = jnp.searchsorted(jnp.cumsum(tallies), jnp.arange(rows * top), side="right").astype(jnp.int32)
    table = items.reshape(top, rows).T
    table = table[jax.random.permutation(jax.random.fold_in(own, 1), rows)]
    offset_by = jax.random.randint(jax.random.fold_in(own, 2), (rows, 1), 0, top)
    return jnp.take_along_axis(table, (jnp.arange(top)[None, :] + offset_by) % top, axis=1)


def portions_of(amount, total, reach, skew, full):
    weights = [(1 << 20) // math.isqrt(standing ** skew) + 1 for standing in range(1, amount + 1)]
    largest = reach if full else min(reach, max(-(-total // amount), total * weights[0] // sum(weights)))
    least = 1 if total - largest >= amount - 1 else 0
    given, rest = [largest] + [least] * (amount - 1), total - largest - least * (amount - 1)
    while rest > 0:
        free = [i for i in range(1, amount) if given[i] < largest] or [i for i in range(1, amount) if given[i] < reach]
        mass, left = sum([weights[i] for i in free]), rest
        for i in free:
            extra = min(reach - given[i], max(1, left * weights[i] // mass), rest)
            given[i] = given[i] + extra
            rest = rest - extra
    return np.array(given)


def centred(rng, shape, width, limit, split=(), kind=jnp.bfloat16):
    values = width * jax.random.normal(rng, shape, jnp.float32)
    if split:
        values = values * shard_levels(rng, shape, split, -0.22, 0.18)
    return jnp.clip(values, -limit, limit).astype(kind)


def setup_inputs(seed: int = 0) -> dict:
    streams_of = jax.random.split(jax.random.key(seed), 5)
    marker_force = centred(streams_of[0], (3, MARKERS), 0.25, 1.5, ((1, 256),), jnp.float32)
    marker_offset = jnp.clip(1.0 * jax.random.uniform(streams_of[1], (3, MARKERS), jnp.float32) ** shard_levels(streams_of[1], (3, MARKERS), ((1, 256),), -0.2, 0.2), 0.0, 1.0)
    marker_cell = draw_marker_cell(jax.random.fold_in(streams_of[4], 71), 0)
    marker_slab_keys = jax.random.split(jax.random.fold_in(streams_of[3], 1), MARKERS // MK_DEV)
    marker_slab_turns = jax.random.permutation(jax.random.fold_in(streams_of[3], 3), MARKERS // MK_DEV)
    marker_slab = jax.vmap(lambda own, number: deal_out(jax.random.fold_in(streams_of[3], 2), own, number, MK_DEV, N_SLAB, 1, CAP, 2))(marker_slab_keys, marker_slab_turns).reshape((MARKERS, 1))
    return {"marker_force": marker_force, "marker_offset": marker_offset, "marker_cell": marker_cell, "marker_slab": marker_slab}


def kernel_weights(fraction):
    return jnp.stack([0.25 * (1.0 + jnp.cos(0.5 * math.pi * jnp.abs(offset_cell - fraction))) for offset_cell in (-1.0, 0.0, 1.0, 2.0)])


def frequency_order():
    levels = SPAN_BLOCKS.bit_length() - 1
    ordering = []
    for position in range(NZ):
        block_id = position // ZS
        flipped = 0
        for section_bit in range(levels):
            flipped = flipped | (((block_id >> section_bit) & 1) << (levels - 1 - section_bit))
        ordering.append(flipped + SPAN_BLOCKS * (position % ZS))
    return np.array(ordering, dtype=np.int32)


def reference(marker_force, marker_offset, marker_cell, marker_slab):
    spans = (jnp.arange(MARKERS, dtype=jnp.int32) // MK_DEV) % SPAN_BLOCKS
    base_x = marker_slab[:, 0] * CX + marker_cell[0]
    base_y = marker_cell[1]
    base_z = spans * ZS + marker_cell[2]
    offsets = jnp.arange(4, dtype=jnp.int32) - 1

    def accumulate(index, field):
        start = index * MK_DEV

        def piece(values):
            return lax.dynamic_slice_in_dim(values, start, MK_DEV, values.ndim - 1)

        force = piece(marker_force)
        offset_now = piece(marker_offset)
        weight_x = kernel_weights(offset_now[0])
        weight_y = kernel_weights(offset_now[1])
        weight_z = kernel_weights(offset_now[2])
        spread = (force[:, None, None, :] * weight_x[None, :, None, :]) * weight_z[None, None, :, :]
        spread = lax.optimization_barrier(spread.astype(jnp.bfloat16)).astype(jnp.float32)
        rounded_y = lax.optimization_barrier(weight_y.astype(jnp.bfloat16)).astype(jnp.float32)
        terms = spread[:, :, :, None, :] * rounded_y[None, None, None, :, :]
        cell_x = piece(base_x)[None, :] + offsets[:, None]
        cell_y = piece(base_y)[None, :] + offsets[:, None]
        cell_z = (piece(base_z)[None, :] + offsets[:, None]) % NZ
        valid_x = (cell_x >= 0) & (cell_x < NX)
        valid_y = (cell_y >= 0) & (cell_y < NY)
        valid = valid_x[:, None, None, :] & valid_y[None, None, :, :]
        terms = jnp.where(valid[None], terms, 0.0)
        terms = jnp.moveaxis(terms, 0, -1)
        index_x = jnp.clip(cell_x, 0, NX - 1)[:, None, None, :]
        index_z = cell_z[None, :, None, :]
        index_y = jnp.clip(cell_y, 0, NY - 1)[None, None, :, :]
        return field.at[index_x, index_z, index_y].add(terms)

    field = lax.fori_loop(0, MARKERS // MK_DEV, accumulate, jnp.zeros((NX, NZ, NY, 3), jnp.float32))
    field = jnp.moveaxis(field, -1, 0)
    spec = jnp.fft.fft(field, axis=2)
    spec = spec[:, :, frequency_order(), :]
    return jnp.stack([jnp.real(spec), jnp.imag(spec)]).astype(jnp.float32)
```

```python
import functools
import math

import jax
import jax.numpy as jnp
import numpy as np
from jax import lax
from jax.experimental import pallas as pl
from jax.experimental.pallas import tpu as pltpu
from jax.sharding import PartitionSpec as P

CX = 2
NY = 128
NZ = 512
SLABS = 32
SPANS = 8
ZS = NZ // SPANS
COUNT = 16384
CAP = 1024
LANES = 128
GROUPS = COUNT // LANES
PIECES = 14
SLOT_HIGH = SLABS * CAP // 256
ROWS_Z = 80
KEPT_Z = 72
ROWS_X = CX + 3
STEP_GROUPS = 16
bf16 = jnp.bfloat16
f32 = jnp.float32
i32 = jnp.int32

NT = (((1,), (1,)), ((), ()))


def one_hot_tile(row, rows):
    sublane = lax.broadcasted_iota(i32, (16, LANES), 0)
    row = jnp.broadcast_to(row, (16, LANES))
    return jnp.where((row & 15) == sublane, row >> 4, -1).astype(f32).astype(bf16)


def bucket_kernel(force, offset, cell, slab, out, spread_a, spread_l, total):
    total[...] = jnp.zeros_like(total)
    bucket = lax.broadcasted_iota(i32, (SLABS, LANES), 0)
    row = lax.broadcasted_iota(i32, (LANES, 2 * LANES), 0)
    col = lax.broadcasted_iota(i32, (LANES, 2 * LANES), 1)
    before = jnp.where((col >= LANES) | (row < col), 1.0, 0.0).astype(bf16)
    zero = jnp.zeros((16, LANES), bf16)
    one = jnp.ones((16, LANES), bf16)

    def step(index, carry):
        owners = slab[pl.ds(pl.multiple_of(index * 8, 8), 8), :]
        member = [bucket == owners[j : j + 1, :] for j in range(8)]
        stacked = jnp.concatenate([jnp.where(m, 1.0, 0.0).astype(bf16) for m in member], axis=0)
        counted = jnp.dot(stacked, before, preferred_element_type=f32)
        for j in range(8):
            part = counted[SLABS * j : SLABS * (j + 1)]
            rank = jnp.sum(
                jnp.where(member[j], part[:, :LANES] + carry, 0.0), axis=0, keepdims=True
            ).astype(i32)
            carry = carry + part[:, LANES:]
            high = owners[j : j + 1, :] * 4 + ((rank >> 7) & 3)
            low = (rank >> 9) * LANES + (rank & 127)
            high_tile = one_hot_tile(high, SLOT_HIGH)
            low_tile = one_hot_tile(low, 256)
            here = pl.ds(pl.multiple_of(index * 8 * LANES + j * LANES, LANES), LANES)
            lanes = slice(j * LANES, (j + 1) * LANES)
            pieces = []
            for source in (force, offset):
                values = source[:, here]
                for c in range(3):
                    whole = jnp.broadcast_to(values[c : c + 1, :], (16, LANES))
                    upper = whole.astype(bf16)
                    pieces.append(upper)
                    pieces.append((whole - upper.astype(f32)).astype(bf16))
            cells = cell[:, here]
            pieces.append(jnp.broadcast_to(cells[1:2, :], (16, LANES)).astype(f32).astype(bf16))
            both = (cells[0:1, :] + 1) * 64 + cells[2:3, :]
            pieces.append(jnp.broadcast_to(both, (16, LANES)).astype(f32).astype(bf16))
            for t in range(SLOT_HIGH // 16):
                hit = high_tile == jnp.asarray(t, bf16)
                for p in range(PIECES):
                    start = p * SLOT_HIGH + t * 16
                    spread_a[start : start + 16, lanes] = jnp.where(hit, pieces[p], zero)
            for t in range(16):
                hit = low_tile == jnp.asarray(t, bf16)
                spread_l[t * 16 : t * 16 + 16, lanes] = jnp.where(hit, one, zero)
        total[...] += lax.dot_general(
            spread_a[...], spread_l[...], NT, preferred_element_type=f32
        )
        return carry

    lax.fori_loop(0, GROUPS // 8, step, jnp.zeros((SLABS, LANES), f32))

    def emit(pair, _):
        def rows(piece):
            start = pl.multiple_of(piece * SLOT_HIGH + pair * 8, 8)
            return total[pl.ds(start, 8), :]

        values = [rows(2 * v) + rows(2 * v + 1) for v in range(6)]
        both = rows(13).astype(i32)
        values.append((both >> 6).astype(f32))
        values.append(rows(12))
        values.append((both & 63).astype(f32))
        for v, value in enumerate(values):
            left, right = value[:, :LANES], value[:, LANES:]
            out[2 * pair, v * 8 : v * 8 + 8, :] = jnp.concatenate([left[0:4], right[0:4]], axis=0)
            out[2 * pair + 1, v * 8 : v * 8 + 8, :] = jnp.concatenate([left[4:8], right[4:8]], axis=0)
        return 0

    lax.fori_loop(0, SLABS // 2, emit, 0)


def bucketed(force, offset, cell, slab):
    return pl.pallas_call(
        bucket_kernel,
        out_shape=jax.ShapeDtypeStruct((SLABS, 72, LANES), f32),
        in_specs=[pl.BlockSpec(memory_space=pltpu.VMEM)] * 4,
        out_specs=pl.BlockSpec(memory_space=pltpu.VMEM),
        scratch_shapes=[
            pltpu.VMEM((PIECES * SLOT_HIGH, 8 * LANES), bf16),
            pltpu.VMEM((256, 8 * LANES), bf16),
            pltpu.VMEM((PIECES * SLOT_HIGH, 256), f32),
        ],
        compiler_params=pltpu.CompilerParams(vmem_limit_bytes=40 * 2**20),
        name="bucket_markers",
    )(force, offset, cell, slab)


def quarter_sine(angle):
    square = angle * angle
    total = jnp.full_like(angle, 1.0 / math.factorial(13))
    for n in (11, 9, 7, 5, 3, 1):
        total = (-1.0) ** ((n - 1) // 2) / math.factorial(n) + square * total
    return angle * total


def spread_kernel(got, own, up, down, table, listed, spread_a, spread_b, total):
    total[...] = jnp.zeros_like(total)
    half_pi = 0.5 * math.pi

    def prepare(source, count):
        def value(v):
            return got[source, v * 8 : v * 8 + 8, :]

        rows = pl.ds(pl.multiple_of(source * 8, 8), 8)
        kind_x = value(6)
        filled = jnp.sum(jnp.where(kind_x > 0.5, 1, 0))

        def waves(fraction):
            return quarter_sine(fraction * half_pi), quarter_sine((1.0 - fraction) * half_pi)

        sine, cosine = waves(value(3))
        weights = [
            0.25 * (1.0 - sine),
            0.25 * (1.0 + cosine),
            0.25 * (1.0 + sine),
            0.25 * (1.0 - cosine),
        ]
        second = kind_x > 1.5
        none = jnp.zeros_like(sine)
        for r in range(ROWS_X):
            at_zero = weights[r] if r < 4 else none
            at_one = weights[r - 1] if r > 0 else none
            table[r, rows, :] = jnp.where(second, at_one, at_zero)
        for number, base in ((0, value(8)), (1, value(7))):
            sine, cosine = waves(value(5 - number))
            base = base.astype(i32)
            odd = (base & 1) == 1
            upper = (base & 2) == 2
            first = jnp.where(odd, -sine, cosine)
            other = jnp.where(odd, cosine, sine)
            table[5 + 2 * number, rows, :] = 0.25 * jnp.where(upper, -first, first)
            table[6 + 2 * number, rows, :] = 0.25 * jnp.where(upper, -other, other)

        def add(r, count):
            listed[count] = source * 8 + r
            return count + 1

        return lax.fori_loop(0, (filled + LANES - 1) // LANES, add, count)

    count = lax.fori_loop(0, SLABS, prepare, jnp.int32(0))
    for extra in range(STEP_GROUPS):
        listed[count + extra] = 0

    sublane = lax.broadcasted_iota(i32, (16, LANES), 0)
    phase = lax.broadcasted_iota(i32, (8, LANES), 0) & 3
    even_z = jnp.where(phase == 1, 1.0, 0.0) - jnp.where(phase == 3, 1.0, 0.0)
    odd_z = jnp.where(phase == 2, 1.0, 0.0) - jnp.where(phase == 0, 1.0, 0.0)
    even_y = jnp.where(phase == 0, 1.0, 0.0) - jnp.where(phase == 2, 1.0, 0.0)
    odd_y = jnp.where(phase == 1, 1.0, 0.0) - jnp.where(phase == 3, 1.0, 0.0)
    zero = jnp.zeros((16, LANES), bf16)

    def met_tile(last):
        above = last - sublane
        return jnp.where((above & 15) < 4, above >> 4, -1).astype(f32).astype(bf16)

    def doubled(value):
        return jnp.concatenate([value, value], axis=0).astype(bf16)

    def step(index, _):
        for j in range(STEP_GROUPS):
            position = index * STEP_GROUPS + j
            group = listed[position]
            source, r = group >> 3, group & 7
            lanes = slice(j * LANES, (j + 1) * LANES)

            def value(v):
                return got[source, pl.ds(v * 8 + r, 1), :]

            def made(v):
                return table[v, pl.ds(group, 1), :]

            keep = jnp.where(position < count, 1.0, 0.0)
            pattern_z = 0.25 + even_z * made(5) + odd_z * made(6)
            pattern_y = 0.25 + even_y * made(7) + odd_y * made(8)
            met_z = met_tile(jnp.broadcast_to(value(8).astype(i32) + 3, (16, LANES)))
            met_y = met_tile(jnp.broadcast_to(value(7).astype(i32) + 2, (16, LANES)))
            planes = [doubled(pattern_z * made(x)) for x in range(ROWS_X)]
            forces = [doubled(pattern_y * (value(c) * keep)) for c in range(3)]
            for t in range(ROWS_Z // 16):
                hit = met_z == jnp.asarray(t, bf16)
                for x in range(ROWS_X):
                    start = x * ROWS_Z + t * 16
                    spread_a[start : start + 16, lanes] = jnp.where(hit, planes[x], zero)
            for t in range(NY // 16):
                hit = met_y == jnp.asarray(t, bf16)
                for c in range(3):
                    start = c * NY + t * 16
                    spread_b[start : start + 16, lanes] = jnp.where(hit, forces[c], zero)
        total[...] += lax.dot_general(
            spread_a[...], spread_b[...], NT, preferred_element_type=f32
        )
        return 0

    lax.fori_loop(0, (count + STEP_GROUPS - 1) // STEP_GROUPS, step, 0)

    down[...] = total[0:KEPT_Z, :]
    for x in range(2):
        own[x] = total[(1 + x) * ROWS_Z : (1 + x) * ROWS_Z + KEPT_Z, :]
        up[x] = total[(3 + x) * ROWS_Z : (3 + x) * ROWS_Z + KEPT_Z, :]


def spread(got):
    block = jax.ShapeDtypeStruct((2, KEPT_Z, 3 * NY), f32)
    return pl.pallas_call(
        spread_kernel,
        out_shape=(block, block, jax.ShapeDtypeStruct((KEPT_Z, 3 * NY), f32)),
        in_specs=[pl.BlockSpec(memory_space=pltpu.VMEM)],
        out_specs=(pl.BlockSpec(memory_space=pltpu.VMEM),) * 3,
        scratch_shapes=[
            pltpu.VMEM((9, SLABS * 8, LANES), f32),
            pltpu.SMEM((SLABS * 8 + STEP_GROUPS,), i32),
            pltpu.VMEM((ROWS_X * ROWS_Z, STEP_GROUPS * LANES), bf16),
            pltpu.VMEM((3 * NY, STEP_GROUPS * LANES), bf16),
            pltpu.VMEM((ROWS_X * ROWS_Z, 3 * NY), f32),
        ],
        compiler_params=pltpu.CompilerParams(vmem_limit_bytes=40 * 2**20),
        name="spread_forces",
    )(got)


def transform_kernel(turns, phases, *refs):
    pieces, out = refs[:-1], refs[-1]
    for x in range(2):
        real = jnp.zeros((KEPT_Z, 3 * NY), f32)
        imag = jnp.zeros((KEPT_Z, 3 * NY), f32)
        for number, piece in enumerate(pieces):
            block = piece[x]
            real = real + block * turns[0, number]
            imag = imag + block * turns[1, number]
        result = jnp.dot(
            phases[...],
            jnp.concatenate([real, imag], axis=0),
            precision=lax.Precision.HIGHEST,
            preferred_element_type=f32,
        )
        for part in range(2):
            for c in range(3):
                out[part, c, x] = result[part * ZS : (part + 1) * ZS, c * NY : (c + 1) * NY]


def transform(turns, phases, pieces):
    return pl.pallas_call(
        transform_kernel,
        out_shape=jax.ShapeDtypeStruct((2, 3, CX, ZS, NY), f32),
        in_specs=[pl.BlockSpec(memory_space=pltpu.SMEM)]
        + [pl.BlockSpec(memory_space=pltpu.VMEM)] * (1 + len(pieces)),
        out_specs=pl.BlockSpec(memory_space=pltpu.VMEM),
        compiler_params=pltpu.CompilerParams(vmem_limit_bytes=40 * 2**20),
        name="fold_and_transform",
    )(turns, phases, *pieces)


def shards(marker_force, marker_offset, marker_cell, marker_slab):
    sent = bucketed(
        marker_force, marker_offset, marker_cell, marker_slab.reshape(GROUPS, LANES)
    )
    got = lax.all_to_all(sent, "slab", split_axis=0, concat_axis=0, tiled=True)
    own, up, down = spread(got)
    upward = [(i, i + 1) for i in range(SLABS - 1)]
    from_below = lax.ppermute(up, "slab", upward)
    from_above = lax.ppermute(down, "slab", [(j, i) for i, j in upward])
    field = own + from_below
    field = jnp.stack([field[0], field[1] + from_above])

    span = lax.axis_index("span")
    residue = ((span & 1) << 2) | (span & 2) | (span >> 2)
    forward = [(i, (i + 1) % SPANS) for i in range(SPANS)]
    backward = [(j, i) for i, j in forward]
    pieces, apart = [field], [0]
    ahead = behind = field
    for hop in range(1, SPANS // 2 + 1):
        ahead = lax.ppermute(ahead, "span", forward)
        pieces.append(ahead)
        apart.append(-hop)
        if hop < SPANS // 2:
            behind = lax.ppermute(behind, "span", backward)
            pieces.append(behind)
            apart.append(hop)
    origin = (span + jnp.asarray(apart, i32)) % SPANS
    turn = (residue * origin % SPANS).astype(f32) * (2.0 * math.pi / SPANS)
    turns = jnp.stack([jnp.cos(turn), -jnp.sin(turn)])
    local = jnp.arange(KEPT_Z, dtype=i32) - 1
    wanted = residue + SPANS * jnp.arange(ZS, dtype=i32)
    angle = (wanted[:, None] * local[None, :] % NZ).astype(f32) * (2.0 * math.pi / NZ)
    cosine, sine = jnp.cos(angle), jnp.sin(angle)
    phases = jnp.concatenate(
        [jnp.concatenate([cosine, sine], axis=1), jnp.concatenate([-sine, cosine], axis=1)], axis=0
    )
    return transform(turns, phases, pieces)


def solution(mesh):
    placed = (
        P(None, ("slab", "span")),
        P(None, ("slab", "span")),
        P(None, ("slab", "span")),
        P(("slab", "span"), None),
    )
    return jax.shard_map(
        shards,
        mesh=mesh,
        in_specs=placed,
        out_specs=P(None, None, "slab", "span", None),
        check_vma=False,
    )
```

```python
import functools
import math

import jax
import jax.numpy as jnp
import numpy as np
from jax import lax
from jax.experimental import pallas as pl
from jax.experimental.pallas import tpu as pltpu
from jax.sharding import PartitionSpec as P

CX = 2
NY = 128
NZ = 512
SLABS = 32
SPANS = 8
ZS = NZ // SPANS
COUNT = 16384
CAP = 1024
LANES = 128
GROUPS = COUNT // LANES
ROWS_Z = 80
KEPT_Z = 72
ROWS_X = CX + 3
STEP_GROUPS = 8
COLS = 256
bf16 = jnp.bfloat16
f32 = jnp.float32
i32 = jnp.int32

NT = (((1,), (1,)), ((), ()))


def one_hot_tile(row, rows_each, sublane):
    apart = 16 // rows_each
    row = jnp.broadcast_to(row, (16, LANES))
    met = (row & (apart - 1)) == sublane // rows_each
    return jnp.where(met, row >> (apart.bit_length() - 1), -1).astype(f32).astype(bf16)


def bucket_kernel(force_in, offset_in, cell_in, slab_in, out, force, offset, cell, slab, placed, wide, bases, firsts, stage, rows_0, rows_1, slots_0, slots_1, sems):
    copies = [
        pltpu.make_async_copy(source, target, sems.at[n])
        for n, (source, target) in enumerate(
            ((slab_in, slab), (force_in, force), (offset_in, offset), (cell_in, cell))
        )
    ]
    for copy in copies:
        copy.start()
    bucket = lax.broadcasted_iota(i32, (SLABS, LANES), 0)
    lane = lax.broadcasted_iota(i32, (SLABS, LANES), 1)
    row = lax.broadcasted_iota(i32, (LANES, 2 * LANES), 0)
    col = lax.broadcasted_iota(i32, (LANES, 2 * LANES), 1)
    before = jnp.where((col >= LANES) | (row < col), 1.0, 0.0).astype(bf16)
    sublane = lax.broadcasted_iota(i32, (16, LANES), 0)
    zero = jnp.zeros((16, LANES), bf16)
    one = jnp.ones((16, LANES), bf16)
    stage[...] = jnp.zeros_like(stage)
    copies[0].wait()

    def count(index, state):
        carry, starts, furthest = state
        chunk_first = carry & -LANES
        owners = slab[pl.ds(pl.multiple_of(index * 8, 8), 8), :]
        member = [bucket == owners[j : j + 1, :] for j in range(8)]
        stacked = jnp.concatenate([jnp.where(m, 1.0, 0.0).astype(bf16) for m in member], axis=0)
        counted = jnp.dot(stacked, before, preferred_element_type=f32)
        ranks, ahead = [], []
        for j in range(8):
            part = counted[SLABS * j : SLABS * (j + 1)]
            within = part[:, :LANES] + (carry & (LANES - 1)).astype(f32)
            ranks.append(jnp.sum(jnp.where(member[j], within, 0.0), axis=0, keepdims=True))
            within = part[:, :LANES] + (carry - chunk_first).astype(f32)
            ahead.append(jnp.sum(jnp.where(member[j], within, 0.0), axis=0, keepdims=True))
            starts = jnp.where(lane == index * 8 + j, carry >> 7, starts)
            carry = carry + part[:, LANES:].astype(i32)
        here = pl.ds(pl.multiple_of(index * 8, 8), 8)
        ahead = jnp.concatenate(ahead, axis=0)
        placed[here, :] = jnp.concatenate(ranks, axis=0).astype(i32)
        wide[here, :] = ahead.astype(i32)
        return carry, starts, jnp.maximum(furthest, ahead)

    none = jnp.zeros((SLABS, LANES), i32)
    _, starts, furthest = lax.fori_loop(
        0, GROUPS // 8, count, (none, none, jnp.zeros((8, LANES), f32)), unroll=4
    )
    windowed = jnp.max(furthest) < 2 * LANES - 0.5
    firsts[...] = starts
    last = pltpu.make_async_copy(firsts, bases, sems.at[4])
    last.start()
    for copy in copies[1:]:
        copy.wait()
    last.wait()

    def valued(g):
        here = pl.ds(pl.multiple_of(g * LANES, LANES), LANES)
        cells = cell[:, here]
        both = (cells[0:1, :] + 1) * ZS + cells[2:3, :]
        return jnp.concatenate(
            [force[:, here], offset[:, here], cells[1:2, :].astype(f32), both.astype(f32)], axis=0
        )

    def group(g):
        values = valued(g)
        values = jnp.concatenate([values, values], axis=0)
        upper = values.astype(bf16)
        lower = (values - upper.astype(f32)).astype(bf16)
        owner_tile = one_hot_tile(slab[pl.ds(g, 1), :], 8, sublane)
        place_tile = one_hot_tile(placed[pl.ds(g, 1), :], 1, sublane)
        rows, slots = [], []
        for t in range(16):
            hit = owner_tile == jnp.asarray(t, bf16)
            rows.append(jnp.concatenate([jnp.where(hit, upper, zero), jnp.where(hit, lower, zero)], axis=1))
            slot = jnp.where(place_tile == jnp.asarray(t, bf16), one, zero)
            slots.append(jnp.concatenate([slot, slot], axis=1))
        return lax.dot_general(
            jnp.concatenate(rows, axis=0), jnp.concatenate(slots, axis=0), NT, preferred_element_type=f32
        )

    def place(g, _):
        moved = group(g)
        for d in range(SLABS):
            first = bases[d, g]
            stage[d, first] += moved[8 * d : 8 * d + 8, :LANES]
            stage[d, first + 1] += moved[8 * d : 8 * d + 8, LANES:]
        return 0

    def build(chunk, rows, slots):
        for j in range(8):
            g = chunk * 8 + j
            lanes = slice(j * LANES, (j + 1) * LANES)
            values = valued(g)
            lower = values - values.astype(bf16).astype(f32)
            values = jnp.concatenate([values, lower], axis=0).astype(bf16)
            owner = jnp.broadcast_to(slab[pl.ds(g, 1), :], (16, LANES)).astype(f32).astype(bf16)
            place_tile = one_hot_tile(wide[pl.ds(g, 1), :], 1, sublane)
            for d in range(SLABS):
                rows[16 * d : 16 * d + 16, lanes] = jnp.where(owner == jnp.asarray(d, bf16), values, zero)
            for t in range(16):
                slots[16 * t : 16 * t + 16, lanes] = jnp.where(
                    place_tile == jnp.asarray(t, bf16), one, zero
                )

    def take(chunk, rows, slots):
        moved = lax.dot_general(rows[...], slots[...], NT, preferred_element_type=f32)
        for d in range(SLABS):
            first = bases[d, chunk * 8]
            both = moved[16 * d : 16 * d + 8] + moved[16 * d + 8 : 16 * d + 16]
            stage[d, first] += both[:, :LANES]
            stage[d, first + 1] += both[:, LANES:]

    @pl.when(windowed)
    def _():
        build(0, rows_0, slots_0)

        def step(index, _):
            build(2 * index + 1, rows_1, slots_1)
            take(2 * index, rows_0, slots_0)
            build(jnp.minimum(2 * index + 2, GROUPS // 8 - 1), rows_0, slots_0)
            take(2 * index + 1, rows_1, slots_1)
            return 0

        lax.fori_loop(0, GROUPS // 16, step, 0)

    @pl.when(jnp.logical_not(windowed))
    def _():
        lax.fori_loop(0, GROUPS, place, 0)

    def emit(d, _):
        is_last = lax.broadcasted_iota(i32, (8, LANES), 0) == 7
        spans_z = []
        for b in range(8):
            values = stage[d, b]
            both = values[7:8, :].astype(i32)
            out[d, b * 8 : b * 8 + 8, :] = jnp.where(
                is_last, jnp.broadcast_to((both >> 6).astype(f32), (8, LANES)), values
            )
            spans_z.append((both & (ZS - 1)).astype(f32))
        out[d, 64:72, :] = jnp.concatenate(spans_z, axis=0)
        return 0

    lax.fori_loop(0, SLABS, emit, 0, unroll=4)


def bucketed(force, offset, cell, slab):
    return pl.pallas_call(
        bucket_kernel,
        out_shape=jax.ShapeDtypeStruct((SLABS, 72, LANES), f32),
        in_specs=[pl.BlockSpec(memory_space=pl.ANY)] * 4,
        out_specs=pl.BlockSpec(memory_space=pltpu.VMEM),
        scratch_shapes=[
            pltpu.VMEM((3, COUNT), f32),
            pltpu.VMEM((3, COUNT), f32),
            pltpu.VMEM((3, COUNT), i32),
            pltpu.VMEM((GROUPS, LANES), i32),
            pltpu.VMEM((GROUPS, LANES), i32),
            pltpu.VMEM((GROUPS, LANES), i32),
            pltpu.SMEM((SLABS, LANES), i32),
            pltpu.VMEM((SLABS, LANES), i32),
            pltpu.VMEM((SLABS, 10, 8, LANES), f32),
            pltpu.VMEM((16 * SLABS, 8 * LANES), bf16),
            pltpu.VMEM((16 * SLABS, 8 * LANES), bf16),
            pltpu.VMEM((256, 8 * LANES), bf16),
            pltpu.VMEM((256, 8 * LANES), bf16),
            pltpu.SemaphoreType.DMA((5,)),
        ],
        compiler_params=pltpu.CompilerParams(vmem_limit_bytes=62 * 2**20),
        name="bucket_markers",
    )(force, offset, cell, slab)


def quarter_sine(angle):
    square = angle * angle
    total = jnp.full_like(angle, 1.0 / math.factorial(13))
    for n in (11, 9, 7, 5, 3, 1):
        total = (-1.0) ** ((n - 1) // 2) / math.factorial(n) + square * total
    return angle * total


def quarter_pattern(cell, shift, sine, cosine):
    row = lax.broadcasted_iota(i32, (8, LANES), 0)
    number = (row - cell + shift) & 3
    wave = jnp.where((number & 1) == 1, cosine, sine)
    return 0.25 + jnp.where(((number + 1) & 2) == 2, wave, -wave)


def spread_kernel(got, own, up, down, listed, rows_0, rows_1, cols_0, cols_1, total):
    total[...] = jnp.zeros_like(total)
    half_pi = 0.5 * math.pi
    for cols in (cols_0, cols_1):
        cols[3 * ROWS_Z :, :] = jnp.zeros((COLS - 3 * ROWS_Z, STEP_GROUPS * LANES), bf16)
    is_last = lax.broadcasted_iota(i32, (8, LANES), 0) == 7

    def enlist(source, count):
        used = jnp.zeros((8, LANES), f32)
        for b in range(8):
            used = used + jnp.where(got[source, b * 8 : b * 8 + 8, :] > 0.5, 1.0, 0.0)
        filled = jnp.sum(jnp.where(is_last, used, 0.0)).astype(i32)
        for b in range(8):
            listed[count + b] = source * 8 + b
        return count + (filled + LANES - 1) // LANES

    count = lax.fori_loop(0, SLABS, enlist, jnp.int32(0), unroll=4)
    listed[count] = 0
    steps = (count + STEP_GROUPS - 1) // STEP_GROUPS
    sublane = lax.broadcasted_iota(i32, (16, LANES), 0)
    zero = jnp.zeros((16, LANES), bf16)

    def met_tile(cell, shift):
        above = jnp.broadcast_to(cell + shift, (16, LANES)) - sublane
        return jnp.where((above & 15) < 4, above >> 4, -1).astype(f32).astype(bf16)

    def doubled(value):
        return jnp.concatenate([value, value], axis=0).astype(bf16)

    def spread_out(row):
        return jnp.broadcast_to(row, (8, LANES))

    def build(index, rows, cols):
        for j in range(STEP_GROUPS):
            position = index * STEP_GROUPS + j
            chosen = listed[jnp.minimum(position, count)]
            source, b = chosen >> 3, chosen & 7
            lanes = slice(j * LANES, (j + 1) * LANES)
            values = got[source, pl.ds(pl.multiple_of(b * 8, 8), 8), :]
            cell_z = got[source, pl.ds(64 + b, 1), :].astype(i32)
            cell_y = values[6:7].astype(i32)
            keep = jnp.where(position < count, 1.0, 0.0)
            sine = quarter_sine(values * half_pi) * 0.25
            cosine = quarter_sine((1.0 - values) * half_pi) * 0.25
            pattern_y = quarter_pattern(cell_y, 1, spread_out(sine[4:5]), spread_out(cosine[4:5]))
            pattern_z = quarter_pattern(cell_z, 0, spread_out(sine[5:6]), spread_out(cosine[5:6]))
            sine_x, cosine_x = spread_out(sine[3:4]), spread_out(cosine[3:4])
            weights = [0.25 - sine_x, 0.25 + cosine_x, 0.25 + sine_x, 0.25 - cosine_x]
            second = spread_out(values[7:8]) > 1.5
            planes = []
            for r in range(ROWS_X):
                at_zero = weights[r] if r < 4 else 0.0
                at_one = weights[r - 1] if r > 0 else 0.0
                planes.append(doubled(pattern_y * jnp.where(second, at_one, at_zero)))
            forces = [doubled(pattern_z * spread_out(values[c : c + 1] * keep)) for c in range(3)]
            met_y = met_tile(cell_y, 2)
            met_z = met_tile(cell_z, 3)
            for t in range(NY // 16):
                hit = met_y == jnp.asarray(t, bf16)
                for x in range(ROWS_X):
                    start = x * NY + t * 16
                    rows[start : start + 16, lanes] = jnp.where(hit, planes[x], zero)
            for t in range(ROWS_Z // 16):
                hit = met_z == jnp.asarray(t, bf16)
                for c in range(3):
                    start = c * ROWS_Z + t * 16
                    cols[start : start + 16, lanes] = jnp.where(hit, forces[c], zero)

    def take(rows, cols):
        total[...] += lax.dot_general(rows[...], cols[...], NT, preferred_element_type=f32)

    build(0, rows_0, cols_0)

    def step(index, _):
        build(2 * index + 1, rows_1, cols_1)
        take(rows_0, cols_0)
        build(2 * index + 2, rows_0, cols_0)
        take(rows_1, cols_1)
        return 0

    lax.fori_loop(0, (steps + 1) // 2, step, 0)

    for x in range(ROWS_X):
        plane = total[x * NY : (x + 1) * NY, :].T
        target = (down, own.at[0], own.at[1], up.at[0], up.at[1])[x]
        for c in range(3):
            target[c * KEPT_Z : (c + 1) * KEPT_Z, :] = plane[c * ROWS_Z : c * ROWS_Z + KEPT_Z, :]


def spread(got):
    block = jax.ShapeDtypeStruct((2, 3 * KEPT_Z, NY), f32)
    return pl.pallas_call(
        spread_kernel,
        out_shape=(block, block, jax.ShapeDtypeStruct((3 * KEPT_Z, NY), f32)),
        in_specs=[pl.BlockSpec(memory_space=pltpu.VMEM)],
        out_specs=(pl.BlockSpec(memory_space=pltpu.VMEM),) * 3,
        scratch_shapes=[
            pltpu.SMEM((SLABS * 8 + 8,), i32),
            pltpu.VMEM((ROWS_X * NY, STEP_GROUPS * LANES), bf16),
            pltpu.VMEM((ROWS_X * NY, STEP_GROUPS * LANES), bf16),
            pltpu.VMEM((COLS, STEP_GROUPS * LANES), bf16),
            pltpu.VMEM((COLS, STEP_GROUPS * LANES), bf16),
            pltpu.VMEM((ROWS_X * NY, COLS), f32),
        ],
        compiler_params=pltpu.CompilerParams(vmem_limit_bytes=40 * 2**20),
        name="spread_forces",
    )(got)


def transform_kernel(turns, phases, *refs):
    pieces, halves, out = refs[: SPANS - 1], refs[SPANS - 1 : SPANS + 1], refs[-1]
    real, imag = [], []
    for x in range(2):
        blocks = [piece[x] for piece in pieces] + [halves[x][...]]
        real.append(sum(block * turns[0, n] for n, block in enumerate(blocks)))
        imag.append(sum(block * turns[1, n] for n, block in enumerate(blocks)))
    for c in range(3):
        rows = slice(c * KEPT_Z, (c + 1) * KEPT_Z)
        folded = jnp.concatenate(
            [jnp.concatenate([part[x][rows] for x in range(2)], axis=1) for part in (real, imag)],
            axis=0,
        )
        result = jnp.dot(
            phases[...], folded, precision=lax.Precision.HIGHEST, preferred_element_type=f32
        )
        for part in range(2):
            for x in range(2):
                out[part, c, x] = result[part * ZS : (part + 1) * ZS, x * NY : (x + 1) * NY]


def transform(turns, phases, pieces):
    return pl.pallas_call(
        transform_kernel,
        out_shape=jax.ShapeDtypeStruct((2, 3, CX, ZS, NY), f32),
        in_specs=[pl.BlockSpec(memory_space=pltpu.SMEM)]
        + [pl.BlockSpec(memory_space=pltpu.VMEM)] * (1 + len(pieces)),
        out_specs=pl.BlockSpec(memory_space=pltpu.VMEM),
        compiler_params=pltpu.CompilerParams(vmem_limit_bytes=40 * 2**20),
        name="fold_and_transform",
    )(turns, phases, *pieces)


def shards(marker_force, marker_offset, marker_cell, marker_slab):
    sent = bucketed(
        marker_force, marker_offset, marker_cell, marker_slab.reshape(GROUPS, LANES)
    )
    got = lax.all_to_all(sent, "slab", split_axis=0, concat_axis=0, tiled=True)
    own, up, down = spread(got)
    upward = [(i, i + 1) for i in range(SLABS - 1)]
    from_below = lax.ppermute(up, "slab", upward)
    from_above = lax.ppermute(down, "slab", [(j, i) for i, j in upward])
    field = own + from_below
    field = jnp.stack([field[0], field[1] + from_above])

    span = lax.axis_index("span")
    residue = ((span & 1) << 2) | (span & 2) | (span >> 2)
    forward = [(i, (i + 1) % SPANS) for i in range(SPANS)]
    backward = [(j, i) for i, j in forward]
    pieces, apart = [field], [0]
    ahead = behind = field
    for hop in range(1, SPANS // 2):
        ahead = lax.ppermute(ahead, "span", forward)
        behind = lax.ppermute(behind, "span", backward)
        pieces += [ahead, behind]
        apart += [-hop, hop]
    pieces.append(lax.ppermute(ahead[0], "span", forward))
    pieces.append(lax.ppermute(behind[1], "span", backward))
    apart.append(SPANS // 2)
    origin = (span + jnp.asarray(apart, i32)) % SPANS
    turn = (residue * origin % SPANS).astype(f32) * (2.0 * math.pi / SPANS)
    turns = jnp.stack([jnp.cos(turn), -jnp.sin(turn)])
    local = jnp.arange(KEPT_Z, dtype=i32) - 1
    wanted = residue + SPANS * jnp.arange(ZS, dtype=i32)
    angle = (wanted[:, None] * local[None, :] % NZ).astype(f32) * (2.0 * math.pi / NZ)
    cosine, sine = jnp.cos(angle), jnp.sin(angle)
    phases = jnp.concatenate(
        [jnp.concatenate([cosine, sine], axis=1), jnp.concatenate([-sine, cosine], axis=1)], axis=0
    )
    return transform(turns, phases, pieces)


def solution(mesh):
    placed = (
        P(None, ("slab", "span")),
        P(None, ("slab", "span")),
        P(None, ("slab", "span")),
        P(("slab", "span"), None),
    )
    return jax.shard_map(
        shards,
        mesh=mesh,
        in_specs=placed,
        out_specs=P(None, None, "slab", "span", None),
        check_vma=False,
    )
```

```python
import functools
import math

import jax
import jax.numpy as jnp
import numpy as np
from jax import lax
from jax.experimental import pallas as pl
from jax.experimental.pallas import tpu as pltpu
from jax.sharding import PartitionSpec as P

CX = 2
NY = 128
NZ = 512
SLABS = 32
SPANS = 8
ZS = NZ // SPANS
COUNT = 16384
CAP = 1024
LANES = 128
GROUPS = COUNT // LANES
ROWS_Z = 80
KEPT_Z = 72
ROWS_X = CX + 3
STEP_GROUPS = 16
COLS = 256
bf16 = jnp.bfloat16
f32 = jnp.float32
i32 = jnp.int32

NT = (((1,), (1,)), ((), ()))


def one_hot_tile(row, rows_each, sublane):
    apart = 16 // rows_each
    row = jnp.broadcast_to(row, (16, LANES))
    met = (row & (apart - 1)) == sublane // rows_each
    return jnp.where(met, row >> (apart.bit_length() - 1), -1).astype(f32).astype(bf16)


def bucket_kernel(force_in, offset_in, cell_in, slab_in, out, force, offset, cell, slab, placed, wide, bases, firsts, stage, rows_0, rows_1, slots_0, slots_1, sems):
    copies = [
        pltpu.make_async_copy(source, target, sems.at[n])
        for n, (source, target) in enumerate(
            ((slab_in, slab), (force_in, force), (offset_in, offset), (cell_in, cell))
        )
    ]
    for copy in copies:
        copy.start()
    bucket = lax.broadcasted_iota(i32, (SLABS, LANES), 0)
    lane = lax.broadcasted_iota(i32, (SLABS, LANES), 1)
    row = lax.broadcasted_iota(i32, (LANES, 2 * LANES), 0)
    col = lax.broadcasted_iota(i32, (LANES, 2 * LANES), 1)
    before = jnp.where((col >= LANES) | (row < col), 1.0, 0.0).astype(bf16)
    sublane = lax.broadcasted_iota(i32, (16, LANES), 0)
    zero = jnp.zeros((16, LANES), bf16)
    one = jnp.ones((16, LANES), bf16)
    stage[...] = jnp.zeros_like(stage)
    copies[0].wait()

    def count(index, state):
        carry, starts, furthest = state
        chunk_first = carry & -LANES
        owners = slab[pl.ds(pl.multiple_of(index * 8, 8), 8), :]
        member = [bucket == owners[j : j + 1, :] for j in range(8)]
        stacked = jnp.concatenate([jnp.where(m, 1.0, 0.0).astype(bf16) for m in member], axis=0)
        counted = jnp.dot(stacked, before, preferred_element_type=f32)
        ranks, ahead = [], []
        for j in range(8):
            part = counted[SLABS * j : SLABS * (j + 1)]
            within = part[:, :LANES] + (carry & (LANES - 1)).astype(f32)
            ranks.append(jnp.sum(jnp.where(member[j], within, 0.0), axis=0, keepdims=True))
            within = part[:, :LANES] + (carry - chunk_first).astype(f32)
            ahead.append(jnp.sum(jnp.where(member[j], within, 0.0), axis=0, keepdims=True))
            starts = jnp.where(lane == index * 8 + j, carry >> 7, starts)
            carry = carry + part[:, LANES:].astype(i32)
        here = pl.ds(pl.multiple_of(index * 8, 8), 8)
        ahead = jnp.concatenate(ahead, axis=0)
        placed[here, :] = jnp.concatenate(ranks, axis=0).astype(i32)
        wide[here, :] = ahead.astype(i32)
        return carry, starts, jnp.maximum(furthest, ahead)

    none = jnp.zeros((SLABS, LANES), i32)
    _, starts, furthest = lax.fori_loop(
        0, GROUPS // 8, count, (none, none, jnp.zeros((8, LANES), f32)), unroll=4
    )
    windowed = jnp.max(furthest) < 2 * LANES - 0.5
    firsts[...] = starts
    last = pltpu.make_async_copy(firsts, bases, sems.at[4])
    last.start()
    for copy in copies[1:]:
        copy.wait()
    last.wait()

    def valued(g):
        here = pl.ds(pl.multiple_of(g * LANES, LANES), LANES)
        cells = cell[:, here]
        both = (cells[0:1, :] + 1) * ZS + cells[2:3, :]
        return jnp.concatenate(
            [force[:, here], offset[:, here], cells[1:2, :].astype(f32), both.astype(f32)], axis=0
        )

    def group(g):
        values = valued(g)
        values = jnp.concatenate([values, values], axis=0)
        upper = values.astype(bf16)
        lower = (values - upper.astype(f32)).astype(bf16)
        owner_tile = one_hot_tile(slab[pl.ds(g, 1), :], 8, sublane)
        place_tile = one_hot_tile(placed[pl.ds(g, 1), :], 1, sublane)
        rows, slots = [], []
        for t in range(16):
            hit = owner_tile == jnp.asarray(t, bf16)
            rows.append(jnp.concatenate([jnp.where(hit, upper, zero), jnp.where(hit, lower, zero)], axis=1))
            slot = jnp.where(place_tile == jnp.asarray(t, bf16), one, zero)
            slots.append(jnp.concatenate([slot, slot], axis=1))
        return lax.dot_general(
            jnp.concatenate(rows, axis=0), jnp.concatenate(slots, axis=0), NT, preferred_element_type=f32
        )

    def place(g, _):
        moved = group(g)
        for d in range(SLABS):
            first = bases[d, g]
            stage[d, first] += moved[8 * d : 8 * d + 8, :LANES]
            stage[d, first + 1] += moved[8 * d : 8 * d + 8, LANES:]
        return 0

    def build(chunk, rows, slots):
        for j in range(8):
            g = chunk * 8 + j
            lanes = slice(j * LANES, (j + 1) * LANES)
            values = valued(g)
            lower = values - values.astype(bf16).astype(f32)
            values = jnp.concatenate([values, lower], axis=0).astype(bf16)
            owner = jnp.broadcast_to(slab[pl.ds(g, 1), :], (16, LANES)).astype(f32).astype(bf16)
            place_tile = one_hot_tile(wide[pl.ds(g, 1), :], 1, sublane)
            for d in range(SLABS):
                rows[16 * d : 16 * d + 16, lanes] = jnp.where(owner == jnp.asarray(d, bf16), values, zero)
            for t in range(16):
                slots[16 * t : 16 * t + 16, lanes] = jnp.where(
                    place_tile == jnp.asarray(t, bf16), one, zero
                )

    def take(chunk, rows, slots):
        moved = lax.dot_general(rows[...], slots[...], NT, preferred_element_type=f32)
        for d in range(SLABS):
            first = bases[d, chunk * 8]
            both = moved[16 * d : 16 * d + 8] + moved[16 * d + 8 : 16 * d + 16]
            stage[d, first] += both[:, :LANES]
            stage[d, first + 1] += both[:, LANES:]

    @pl.when(windowed)
    def _():
        build(0, rows_0, slots_0)

        def step(index, _):
            build(2 * index + 1, rows_1, slots_1)
            take(2 * index, rows_0, slots_0)
            build(jnp.minimum(2 * index + 2, GROUPS // 8 - 1), rows_0, slots_0)
            take(2 * index + 1, rows_1, slots_1)
            return 0

        lax.fori_loop(0, GROUPS // 16, step, 0)

    @pl.when(jnp.logical_not(windowed))
    def _():
        lax.fori_loop(0, GROUPS, place, 0)

    def emit(d, _):
        is_last = lax.broadcasted_iota(i32, (8, LANES), 0) == 7
        spans_z = []
        for b in range(8):
            values = stage[d, b]
            both = values[7:8, :].astype(i32)
            out[d, b * 8 : b * 8 + 8, :] = jnp.where(
                is_last, jnp.broadcast_to((both >> 6).astype(f32), (8, LANES)), values
            )
            spans_z.append((both & (ZS - 1)).astype(f32))
        out[d, 64:72, :] = jnp.concatenate(spans_z, axis=0)
        return 0

    lax.fori_loop(0, SLABS, emit, 0, unroll=4)


def bucketed(force, offset, cell, slab):
    return pl.pallas_call(
        bucket_kernel,
        out_shape=jax.ShapeDtypeStruct((SLABS, 72, LANES), f32),
        in_specs=[pl.BlockSpec(memory_space=pl.ANY)] * 4,
        out_specs=pl.BlockSpec(memory_space=pltpu.VMEM),
        scratch_shapes=[
            pltpu.VMEM((3, COUNT), f32),
            pltpu.VMEM((3, COUNT), f32),
            pltpu.VMEM((3, COUNT), i32),
            pltpu.VMEM((GROUPS, LANES), i32),
            pltpu.VMEM((GROUPS, LANES), i32),
            pltpu.VMEM((GROUPS, LANES), i32),
            pltpu.SMEM((SLABS, LANES), i32),
            pltpu.VMEM((SLABS, LANES), i32),
            pltpu.VMEM((SLABS, 10, 8, LANES), f32),
            pltpu.VMEM((16 * SLABS, 8 * LANES), bf16),
            pltpu.VMEM((16 * SLABS, 8 * LANES), bf16),
            pltpu.VMEM((256, 8 * LANES), bf16),
            pltpu.VMEM((256, 8 * LANES), bf16),
            pltpu.SemaphoreType.DMA((5,)),
        ],
        compiler_params=pltpu.CompilerParams(vmem_limit_bytes=62 * 2**20),
        name="bucket_markers",
    )(force, offset, cell, slab)


SINE_TERMS = (
    0.39269908001633835,
    -0.1614909401096207,
    0.019922480650110423,
    -0.0011685376672223781,
    3.791877944380962e-05,
)


def quarter_sine(turn):
    square = turn * turn
    total = SINE_TERMS[-1]
    for term in SINE_TERMS[-2::-1]:
        total = term + square * total
    return turn * total


def quarter_pattern(above, sine, cosine):
    wave = jnp.where((above & 1) == 1, sine, cosine)
    return 0.25 + jnp.where(((above + 1) & 2) == 2, wave, -wave)


def spread_kernel(got, own, up, down, listed, rows_0, rows_1, cols_0, cols_1, total):
    total[...] = jnp.zeros_like(total)
    for cols in (cols_0, cols_1):
        cols[3 * ROWS_Z :, :] = jnp.zeros((COLS - 3 * ROWS_Z, STEP_GROUPS * LANES), bf16)
    row = lax.broadcasted_iota(i32, (8, LANES), 0)
    is_last = row == 7
    is_offset = (row >= 3) & (row < 6)

    def enlist(source, count):
        used = jnp.zeros((8, LANES), f32)
        for b in range(8):
            used = used + jnp.where(got[source, b * 8 : b * 8 + 8, :] > 0.5, 1.0, 0.0)
        filled = jnp.sum(jnp.where(is_last, used, 0.0)).astype(i32)
        for b in range(8):
            listed[count + b] = source * 8 + b
        return count + (filled + LANES - 1) // LANES

    count = lax.fori_loop(0, SLABS, enlist, jnp.int32(0), unroll=4)
    listed[count] = 0
    steps = (count + STEP_GROUPS - 1) // STEP_GROUPS
    sublane = lax.broadcasted_iota(i32, (16, LANES), 0)
    zero = jnp.zeros((16, LANES), bf16)

    def met_tile(above):
        above = above.astype(jnp.int16)
        return jnp.where((above & 15) < 4, above >> 4, jnp.int16(-1))

    def doubled(value):
        return jnp.concatenate([value, value], axis=0).astype(bf16)

    def spread_out(row):
        return jnp.broadcast_to(row, (8, LANES))

    def build(index, rows, cols):
        for j in range(STEP_GROUPS):
            position = index * STEP_GROUPS + j
            chosen = listed[jnp.minimum(position, count)]
            source, b = chosen >> 3, chosen & 7
            lanes = slice(j * LANES, (j + 1) * LANES)
            values = got[source, pl.ds(pl.multiple_of(b * 8, 8), 8), :]
            cell_z = got[source, pl.ds(64 + b, 1), :].astype(i32)
            cell_y = values[6:7].astype(i32)
            keep = jnp.where(position < count, 1.0, 0.0)
            turn = jnp.where(is_offset, values, 1.0 - pltpu.roll(values, 4, 0))
            wave = quarter_sine(turn)
            above_y = jnp.broadcast_to(cell_y + 2, (16, LANES)) - sublane
            above_z = jnp.broadcast_to(cell_z + 3, (16, LANES)) - sublane
            pattern_y = quarter_pattern(above_y[:8], spread_out(wave[4:5]), spread_out(wave[0:1]))
            pattern_z = keep * quarter_pattern(
                above_z[:8], spread_out(wave[5:6]), spread_out(wave[1:2])
            )
            sine_x, cosine_x = spread_out(wave[3:4]), spread_out(wave[7:8])
            weights = [0.25 - sine_x, 0.25 + cosine_x, 0.25 + sine_x, 0.25 - cosine_x]
            second = spread_out(values[7:8]) > 1.5
            planes = []
            for r in range(ROWS_X):
                at_zero = weights[r] if r < 4 else 0.0
                at_one = weights[r - 1] if r > 0 else 0.0
                planes.append(doubled(pattern_y * jnp.where(second, at_one, at_zero)))
            forces = [doubled(pattern_z * spread_out(values[c : c + 1])) for c in range(3)]
            met_y = met_tile(above_y)
            met_z = met_tile(above_z)
            for t in range(NY // 16):
                hit = met_y == jnp.int16(t)
                for x in range(ROWS_X):
                    start = x * NY + t * 16
                    rows[start : start + 16, lanes] = jnp.where(hit, planes[x], zero)
            for t in range(ROWS_Z // 16):
                hit = met_z == jnp.int16(t)
                for c in range(3):
                    start = c * ROWS_Z + t * 16
                    cols[start : start + 16, lanes] = jnp.where(hit, forces[c], zero)

    def take(rows, cols):
        total[...] += lax.dot_general(rows[...], cols[...], NT, preferred_element_type=f32)

    build(0, rows_0, cols_0)

    def step(index, _):
        build(2 * index + 1, rows_1, cols_1)
        take(rows_0, cols_0)
        build(2 * index + 2, rows_0, cols_0)
        take(rows_1, cols_1)
        return 0

    lax.fori_loop(0, (steps + 1) // 2, step, 0)

    for x in range(ROWS_X):
        plane = total[x * NY : (x + 1) * NY, :].T
        target = (down, own.at[0], own.at[1], up.at[0], up.at[1])[x]
        for c in range(3):
            target[c * KEPT_Z : (c + 1) * KEPT_Z, :] = plane[c * ROWS_Z : c * ROWS_Z + KEPT_Z, :]


def spread(got):
    block = jax.ShapeDtypeStruct((2, 3 * KEPT_Z, NY), f32)
    return pl.pallas_call(
        spread_kernel,
        out_shape=(block, block, jax.ShapeDtypeStruct((3 * KEPT_Z, NY), f32)),
        in_specs=[pl.BlockSpec(memory_space=pltpu.VMEM)],
        out_specs=(pl.BlockSpec(memory_space=pltpu.VMEM),) * 3,
        scratch_shapes=[
            pltpu.SMEM((SLABS * 8 + 8,), i32),
            pltpu.VMEM((ROWS_X * NY, STEP_GROUPS * LANES), bf16),
            pltpu.VMEM((ROWS_X * NY, STEP_GROUPS * LANES), bf16),
            pltpu.VMEM((COLS, STEP_GROUPS * LANES), bf16),
            pltpu.VMEM((COLS, STEP_GROUPS * LANES), bf16),
            pltpu.VMEM((ROWS_X * NY, COLS), f32),
        ],
        compiler_params=pltpu.CompilerParams(vmem_limit_bytes=40 * 2**20),
        name="spread_forces",
    )(got)


def transform_kernel(turns, phases, *refs):
    out = refs[-1]
    real, imag = [], []
    for x in range(2):
        blocks = [piece[...] for piece in refs[x:-1:2]]
        real.append(sum(block * turns[0, n] for n, block in enumerate(blocks)))
        imag.append(sum(block * turns[1, n] for n, block in enumerate(blocks)))
    for c in range(3):
        rows = slice(c * KEPT_Z, (c + 1) * KEPT_Z)
        folded = jnp.concatenate(
            [jnp.concatenate([part[x][rows] for x in range(2)], axis=1) for part in (real, imag)],
            axis=0,
        )
        result = jnp.dot(
            phases[...], folded, precision=lax.Precision.HIGHEST, preferred_element_type=f32
        )
        for part in range(2):
            for x in range(2):
                out[part, c, x] = result[part * ZS : (part + 1) * ZS, x * NY : (x + 1) * NY]


def transform(turns, phases, pieces):
    return pl.pallas_call(
        transform_kernel,
        out_shape=jax.ShapeDtypeStruct((2, 3, CX, ZS, NY), f32),
        in_specs=[pl.BlockSpec(memory_space=pltpu.SMEM)]
        + [pl.BlockSpec(memory_space=pltpu.VMEM)] * (1 + len(pieces)),
        out_specs=pl.BlockSpec(memory_space=pltpu.VMEM),
        compiler_params=pltpu.CompilerParams(vmem_limit_bytes=40 * 2**20),
        name="fold_and_transform",
    )(turns, phases, *pieces)


def shards(marker_force, marker_offset, marker_cell, marker_slab):
    sent = bucketed(
        marker_force, marker_offset, marker_cell, marker_slab.reshape(GROUPS, LANES)
    )
    got = lax.all_to_all(sent, "slab", split_axis=0, concat_axis=0, tiled=True)
    own, up, down = spread(got)
    upward = [(i, i + 1) for i in range(SLABS - 1)]
    from_below = lax.ppermute(up, "slab", upward)
    from_above = lax.ppermute(down, "slab", [(j, i) for i, j in upward])
    field = own + from_below
    field = jnp.stack([field[0], field[1] + from_above])

    span = lax.axis_index("span")
    residue = ((span & 1) << 2) | (span & 2) | (span >> 2)
    forward = [(i, (i + 1) % SPANS) for i in range(SPANS)]
    backward = [(j, i) for i, j in forward]
    pieces, apart = [field[0], field[1]], [0]
    ahead, behind = [field[0], field[1]], [field[0], field[1]]
    for hop in range(1, SPANS // 2):
        for x in range(2):
            ahead[x] = lax.ppermute(ahead[x], "span", forward)
            behind[x] = lax.ppermute(behind[x], "span", backward)
        pieces += ahead + behind
        apart += [-hop, hop]
    pieces.append(lax.ppermute(ahead[0], "span", forward))
    pieces.append(lax.ppermute(behind[1], "span", backward))
    apart.append(SPANS // 2)
    origin = (span + jnp.asarray(apart, i32)) % SPANS
    turn = (residue * origin % SPANS).astype(f32) * (2.0 * math.pi / SPANS)
    turns = jnp.stack([jnp.cos(turn), -jnp.sin(turn)])
    local = jnp.arange(KEPT_Z, dtype=i32) - 1
    wanted = residue + SPANS * jnp.arange(ZS, dtype=i32)
    angle = (wanted[:, None] * local[None, :] % NZ).astype(f32) * (2.0 * math.pi / NZ)
    cosine, sine = jnp.cos(angle), jnp.sin(angle)
    phases = jnp.concatenate(
        [jnp.concatenate([cosine, sine], axis=1), jnp.concatenate([-sine, cosine], axis=1)], axis=0
    )
    return transform(turns, phases, pieces)


def solution(mesh):
    placed = (
        P(None, ("slab", "span")),
        P(None, ("slab", "span")),
        P(None, ("slab", "span")),
        P(("slab", "span"), None),
    )
    return jax.shard_map(
        shards,
        mesh=mesh,
        in_specs=placed,
        out_specs=P(None, None, "slab", "span", None),
        check_vma=False,
    )
```

```python
import functools
import math

import jax
import jax.numpy as jnp
import numpy as np
from jax import lax
from jax.experimental import pallas as pl
from jax.experimental.pallas import tpu as pltpu
from jax.sharding import PartitionSpec as P

CX = 2
NY = 128
NZ = 512
SLABS = 32
SPANS = 8
ZS = NZ // SPANS
COUNT = 16384
CAP = 1024
LANES = 128
GROUPS = COUNT // LANES
ROWS_Z = 80
KEPT_Z = 72
ROWS_X = CX + 3
STEP_GROUPS = 16
COLS = 256
bf16 = jnp.bfloat16
f32 = jnp.float32
i32 = jnp.int32

NT = (((1,), (1,)), ((), ()))


def one_hot_tile(row, rows_each, sublane):
    apart = 16 // rows_each
    row = jnp.broadcast_to(row, (16, LANES))
    met = (row & (apart - 1)) == sublane // rows_each
    return jnp.where(met, row >> (apart.bit_length() - 1), -1).astype(f32).astype(bf16)


def bucket_kernel(force_in, offset_in, cell_in, slab_in, out, force, offset, cell, slab, placed, wide, bases, firsts, stage, rows_0, rows_1, slots_0, slots_1, sems):
    copies = [
        pltpu.make_async_copy(source, target, sems.at[n])
        for n, (source, target) in enumerate(
            ((slab_in, slab), (force_in, force), (offset_in, offset), (cell_in, cell))
        )
    ]
    for copy in copies:
        copy.start()
    bucket = lax.broadcasted_iota(i32, (SLABS, LANES), 0)
    lane = lax.broadcasted_iota(i32, (SLABS, LANES), 1)
    row = lax.broadcasted_iota(i32, (LANES, 2 * LANES), 0)
    col = lax.broadcasted_iota(i32, (LANES, 2 * LANES), 1)
    before = jnp.where((col >= LANES) | (row < col), 1.0, 0.0).astype(bf16)
    sublane = lax.broadcasted_iota(i32, (16, LANES), 0)
    zero = jnp.zeros((16, LANES), bf16)
    one = jnp.ones((16, LANES), bf16)
    stage[...] = jnp.zeros_like(stage)
    copies[0].wait()

    def count(index, state):
        carry, starts, furthest = state
        chunk_first = carry & -LANES
        owners = slab[pl.ds(pl.multiple_of(index * 8, 8), 8), :]
        member = [bucket == owners[j : j + 1, :] for j in range(8)]
        stacked = jnp.concatenate([jnp.where(m, 1.0, 0.0).astype(bf16) for m in member], axis=0)
        counted = jnp.dot(stacked, before, preferred_element_type=f32)
        ranks, ahead = [], []
        for j in range(8):
            part = counted[SLABS * j : SLABS * (j + 1)]
            within = part[:, :LANES] + (carry & (LANES - 1)).astype(f32)
            ranks.append(jnp.sum(jnp.where(member[j], within, 0.0), axis=0, keepdims=True))
            within = part[:, :LANES] + (carry - chunk_first).astype(f32)
            ahead.append(jnp.sum(jnp.where(member[j], within, 0.0), axis=0, keepdims=True))
            starts = jnp.where(lane == index * 8 + j, carry >> 7, starts)
            carry = carry + part[:, LANES:].astype(i32)
        here = pl.ds(pl.multiple_of(index * 8, 8), 8)
        ahead = jnp.concatenate(ahead, axis=0)
        placed[here, :] = jnp.concatenate(ranks, axis=0).astype(i32)
        wide[here, :] = ahead.astype(i32)
        return carry, starts, jnp.maximum(furthest, ahead)

    none = jnp.zeros((SLABS, LANES), i32)
    _, starts, furthest = lax.fori_loop(
        0, GROUPS // 8, count, (none, none, jnp.zeros((8, LANES), f32)), unroll=4
    )
    windowed = jnp.max(furthest) < 2 * LANES - 0.5
    firsts[...] = starts
    last = pltpu.make_async_copy(firsts, bases, sems.at[4])
    last.start()
    for copy in copies[1:]:
        copy.wait()
    last.wait()

    def valued(g):
        here = pl.ds(pl.multiple_of(g * LANES, LANES), LANES)
        cells = cell[:, here]
        both = (cells[0:1, :] + 1) * ZS + cells[2:3, :]
        return jnp.concatenate(
            [force[:, here], offset[:, here], cells[1:2, :].astype(f32), both.astype(f32)], axis=0
        )

    def group(g):
        values = valued(g)
        values = jnp.concatenate([values, values], axis=0)
        upper = values.astype(bf16)
        lower = (values - upper.astype(f32)).astype(bf16)
        owner_tile = one_hot_tile(slab[pl.ds(g, 1), :], 8, sublane)
        place_tile = one_hot_tile(placed[pl.ds(g, 1), :], 1, sublane)
        rows, slots = [], []
        for t in range(16):
            hit = owner_tile == jnp.asarray(t, bf16)
            rows.append(jnp.concatenate([jnp.where(hit, upper, zero), jnp.where(hit, lower, zero)], axis=1))
            slot = jnp.where(place_tile == jnp.asarray(t, bf16), one, zero)
            slots.append(jnp.concatenate([slot, slot], axis=1))
        return lax.dot_general(
            jnp.concatenate(rows, axis=0), jnp.concatenate(slots, axis=0), NT, preferred_element_type=f32
        )

    def place(g, _):
        moved = group(g)
        for d in range(SLABS):
            first = bases[d, g]
            stage[d, first] += moved[8 * d : 8 * d + 8, :LANES]
            stage[d, first + 1] += moved[8 * d : 8 * d + 8, LANES:]
        return 0

    def build(chunk, rows, slots):
        for j in range(8):
            g = chunk * 8 + j
            lanes = slice(j * LANES, (j + 1) * LANES)
            values = valued(g)
            lower = values - values.astype(bf16).astype(f32)
            values = jnp.concatenate([values, lower], axis=0).astype(bf16)
            owner = jnp.broadcast_to(slab[pl.ds(g, 1), :], (16, LANES)).astype(f32).astype(bf16)
            place_tile = one_hot_tile(wide[pl.ds(g, 1), :], 1, sublane)
            for d in range(SLABS):
                rows[16 * d : 16 * d + 16, lanes] = jnp.where(owner == jnp.asarray(d, bf16), values, zero)
            for t in range(16):
                slots[16 * t : 16 * t + 16, lanes] = jnp.where(
                    place_tile == jnp.asarray(t, bf16), one, zero
                )

    def take(chunk, rows, slots):
        moved = lax.dot_general(rows[...], slots[...], NT, preferred_element_type=f32)
        for d in range(SLABS):
            first = bases[d, chunk * 8]
            both = moved[16 * d : 16 * d + 8] + moved[16 * d + 8 : 16 * d + 16]
            stage[d, first] += both[:, :LANES]
            stage[d, first + 1] += both[:, LANES:]

    @pl.when(windowed)
    def _():
        build(0, rows_0, slots_0)

        def step(index, _):
            build(2 * index + 1, rows_1, slots_1)
            take(2 * index, rows_0, slots_0)
            build(jnp.minimum(2 * index + 2, GROUPS // 8 - 1), rows_0, slots_0)
            take(2 * index + 1, rows_1, slots_1)
            return 0

        lax.fori_loop(0, GROUPS // 16, step, 0)

    @pl.when(jnp.logical_not(windowed))
    def _():
        lax.fori_loop(0, GROUPS, place, 0)

    def emit(d, _):
        is_last = lax.broadcasted_iota(i32, (8, LANES), 0) == 7
        spans_z = []
        for b in range(8):
            values = stage[d, b]
            both = values[7:8, :].astype(i32)
            out[d, b * 8 : b * 8 + 8, :] = jnp.where(
                is_last, jnp.broadcast_to((both >> 6).astype(f32), (8, LANES)), values
            )
            spans_z.append((both & (ZS - 1)).astype(f32))
        out[d, 64:72, :] = jnp.concatenate(spans_z, axis=0)
        return 0

    lax.fori_loop(0, SLABS, emit, 0, unroll=4)


def bucketed(force, offset, cell, slab):
    return pl.pallas_call(
        bucket_kernel,
        out_shape=jax.ShapeDtypeStruct((SLABS, 72, LANES), f32),
        in_specs=[pl.BlockSpec(memory_space=pl.ANY)] * 4,
        out_specs=pl.BlockSpec(memory_space=pltpu.VMEM),
        scratch_shapes=[
            pltpu.VMEM((3, COUNT), f32),
            pltpu.VMEM((3, COUNT), f32),
            pltpu.VMEM((3, COUNT), i32),
            pltpu.VMEM((GROUPS, LANES), i32),
            pltpu.VMEM((GROUPS, LANES), i32),
            pltpu.VMEM((GROUPS, LANES), i32),
            pltpu.SMEM((SLABS, LANES), i32),
            pltpu.VMEM((SLABS, LANES), i32),
            pltpu.VMEM((SLABS, 10, 8, LANES), f32),
            pltpu.VMEM((16 * SLABS, 8 * LANES), bf16),
            pltpu.VMEM((16 * SLABS, 8 * LANES), bf16),
            pltpu.VMEM((256, 8 * LANES), bf16),
            pltpu.VMEM((256, 8 * LANES), bf16),
            pltpu.SemaphoreType.DMA((5,)),
        ],
        compiler_params=pltpu.CompilerParams(vmem_limit_bytes=62 * 2**20),
        name="bucket_markers",
    )(force, offset, cell, slab)


SINE_TERMS = (
    0.39269908001633835,
    -0.1614909401096207,
    0.019922480650110423,
    -0.0011685376672223781,
    3.791877944380962e-05,
)


def quarter_sine(turn):
    square = turn * turn
    total = SINE_TERMS[-1]
    for term in SINE_TERMS[-2::-1]:
        total = term + square * total
    return turn * total


def quarter_pattern(above, sine, cosine):
    wave = jnp.where((above & 1) == 1, sine, cosine)
    return 0.25 + jnp.where(((above + 1) & 2) == 2, wave, -wave)


def spread_kernel(got, own, up, down, listed, rows_0, rows_1, cols_0, cols_1, total):
    total[...] = jnp.zeros_like(total)
    for cols in (cols_0, cols_1):
        cols[3 * ROWS_Z :, :] = jnp.zeros((COLS - 3 * ROWS_Z, STEP_GROUPS * LANES), bf16)
    row = lax.broadcasted_iota(i32, (8, LANES), 0)
    is_last = row == 7
    is_offset = (row >= 3) & (row < 6)

    def enlist(source, count):
        used = jnp.zeros((8, LANES), f32)
        for b in range(8):
            used = used + jnp.where(got[source, b * 8 : b * 8 + 8, :] > 0.5, 1.0, 0.0)
        filled = jnp.sum(jnp.where(is_last, used, 0.0)).astype(i32)
        for b in range(8):
            listed[count + b] = source * 8 + b
        return count + (filled + LANES - 1) // LANES

    count = lax.fori_loop(0, SLABS, enlist, jnp.int32(0), unroll=4)
    listed[count] = 0
    steps = (count + STEP_GROUPS - 1) // STEP_GROUPS
    sublane = lax.broadcasted_iota(i32, (16, LANES), 0)
    zero = jnp.zeros((16, LANES), bf16)

    def met_tile(above):
        above = above.astype(jnp.int16)
        return jnp.where((above & 15) < 4, above >> 4, jnp.int16(-1))

    def doubled(value):
        return jnp.concatenate([value, value], axis=0).astype(bf16)

    def spread_out(row):
        return jnp.broadcast_to(row, (8, LANES))

    def build(index, rows, cols):
        for j in range(STEP_GROUPS):
            position = index * STEP_GROUPS + j
            chosen = listed[jnp.minimum(position, count)]
            source, b = chosen >> 3, chosen & 7
            lanes = slice(j * LANES, (j + 1) * LANES)
            values = got[source, pl.ds(pl.multiple_of(b * 8, 8), 8), :]
            cell_z = got[source, pl.ds(64 + b, 1), :].astype(i32)
            cell_y = values[6:7].astype(i32)
            keep = jnp.where(position < count, 1.0, 0.0)
            turn = jnp.where(is_offset, values, 1.0 - pltpu.roll(values, 4, 0))
            wave = quarter_sine(turn)
            above_y = jnp.broadcast_to(cell_y + 2, (16, LANES)) - sublane
            above_z = jnp.broadcast_to(cell_z + 3, (16, LANES)) - sublane
            pattern_y = quarter_pattern(above_y[:8], spread_out(wave[4:5]), spread_out(wave[0:1]))
            pattern_z = keep * quarter_pattern(
                above_z[:8], spread_out(wave[5:6]), spread_out(wave[1:2])
            )
            sine_x, cosine_x = spread_out(wave[3:4]), spread_out(wave[7:8])
            weights = [0.25 - sine_x, 0.25 + cosine_x, 0.25 + sine_x, 0.25 - cosine_x]
            second = spread_out(values[7:8]) > 1.5
            planes = []
            for r in range(ROWS_X):
                at_zero = weights[r] if r < 4 else 0.0
                at_one = weights[r - 1] if r > 0 else 0.0
                planes.append(doubled(pattern_y * jnp.where(second, at_one, at_zero)))
            forces = [doubled(pattern_z * spread_out(values[c : c + 1])) for c in range(3)]
            met_y = met_tile(above_y)
            met_z = met_tile(above_z)
            for t in range(NY // 16):
                hit = met_y == jnp.int16(t)
                for x in range(ROWS_X):
                    start = x * NY + t * 16
                    rows[start : start + 16, lanes] = jnp.where(hit, planes[x], zero)
            for t in range(ROWS_Z // 16):
                hit = met_z == jnp.int16(t)
                for c in range(3):
                    start = c * ROWS_Z + t * 16
                    cols[start : start + 16, lanes] = jnp.where(hit, forces[c], zero)

    def take(rows, cols):
        total[...] += lax.dot_general(rows[...], cols[...], NT, preferred_element_type=f32)

    build(0, rows_0, cols_0)

    def step(index, _):
        build(2 * index + 1, rows_1, cols_1)
        take(rows_0, cols_0)
        build(2 * index + 2, rows_0, cols_0)
        take(rows_1, cols_1)
        return 0

    lax.fori_loop(0, (steps + 1) // 2, step, 0)

    for x in range(ROWS_X):
        plane = total[x * NY : (x + 1) * NY, :].T
        target = (down, own.at[0], own.at[1], up.at[0], up.at[1])[x]
        for c in range(3):
            target[c * KEPT_Z : (c + 1) * KEPT_Z, :] = plane[c * ROWS_Z : c * ROWS_Z + KEPT_Z, :]


def spread(got):
    block = jax.ShapeDtypeStruct((2, 3 * KEPT_Z, NY), f32)
    return pl.pallas_call(
        spread_kernel,
        out_shape=(block, block, jax.ShapeDtypeStruct((3 * KEPT_Z, NY), f32)),
        in_specs=[pl.BlockSpec(memory_space=pltpu.VMEM)],
        out_specs=(pl.BlockSpec(memory_space=pltpu.VMEM),) * 3,
        scratch_shapes=[
            pltpu.SMEM((SLABS * 8 + 8,), i32),
            pltpu.VMEM((ROWS_X * NY, STEP_GROUPS * LANES), bf16),
            pltpu.VMEM((ROWS_X * NY, STEP_GROUPS * LANES), bf16),
            pltpu.VMEM((COLS, STEP_GROUPS * LANES), bf16),
            pltpu.VMEM((COLS, STEP_GROUPS * LANES), bf16),
            pltpu.VMEM((ROWS_X * NY, COLS), f32),
        ],
        compiler_params=pltpu.CompilerParams(vmem_limit_bytes=40 * 2**20),
        name="spread_forces",
    )(got)


def transform_kernel(turns, phases, *refs):
    out = refs[-1]
    real, imag = [], []
    for x in range(2):
        blocks = [piece[...] for piece in refs[x:-1:2]]
        real.append(sum(block * turns[0, n] for n, block in enumerate(blocks)))
        imag.append(sum(block * turns[1, n] for n, block in enumerate(blocks)))
    for c in range(3):
        rows = slice(c * KEPT_Z, (c + 1) * KEPT_Z)
        folded = jnp.concatenate(
            [jnp.concatenate([part[x][rows] for x in range(2)], axis=1) for part in (real, imag)],
            axis=0,
        )
        result = jnp.dot(
            phases[...], folded, precision=lax.Precision.HIGHEST, preferred_element_type=f32
        )
        for part in range(2):
            for x in range(2):
                out[part, c, x] = result[part * ZS : (part + 1) * ZS, x * NY : (x + 1) * NY]


def transform(turns, phases, pieces):
    return pl.pallas_call(
        transform_kernel,
        out_shape=jax.ShapeDtypeStruct((2, 3, CX, ZS, NY), f32),
        in_specs=[pl.BlockSpec(memory_space=pltpu.SMEM)]
        + [pl.BlockSpec(memory_space=pltpu.VMEM)] * (1 + len(pieces)),
        out_specs=pl.BlockSpec(memory_space=pltpu.VMEM),
        compiler_params=pltpu.CompilerParams(vmem_limit_bytes=40 * 2**20),
        name="fold_and_transform",
    )(turns, phases, *pieces)


def shards(marker_force, marker_offset, marker_cell, marker_slab):
    sent = bucketed(
        marker_force, marker_offset, marker_cell, marker_slab.reshape(GROUPS, LANES)
    )
    got = lax.all_to_all(sent, "slab", split_axis=0, concat_axis=0, tiled=True)
    own, up, down = spread(got)
    upward = [(i, i + 1) for i in range(SLABS - 1)]
    from_below = lax.ppermute(up, "slab", upward)
    from_above = lax.ppermute(down, "slab", [(j, i) for i, j in upward])
    field = own + from_below
    field = jnp.stack([field[0], field[1] + from_above])

    span = lax.axis_index("span")
    residue = ((span & 1) << 2) | (span & 2) | (span >> 2)
    forward = [(i, (i + 1) % SPANS) for i in range(SPANS)]
    backward = [(j, i) for i, j in forward]
    pieces, apart = [field[0], field[1]], [0]
    ahead, behind = [field[0], field[1]], [field[0], field[1]]
    for hop in range(1, SPANS // 2):
        ahead[0] = lax.ppermute(ahead[0], "span", forward)
        behind[1] = lax.ppermute(behind[1], "span", backward)
        ahead[1] = lax.ppermute(ahead[1], "span", forward)
        behind[0] = lax.ppermute(behind[0], "span", backward)
        pieces += ahead + behind
        apart += [-hop, hop]
    pieces.append(lax.ppermute(ahead[0], "span", forward))
    pieces.append(lax.ppermute(behind[1], "span", backward))
    apart.append(SPANS // 2)
    origin = (span + jnp.asarray(apart, i32)) % SPANS
    turn = (residue * origin % SPANS).astype(f32) * (2.0 * math.pi / SPANS)
    turns = jnp.stack([jnp.cos(turn), -jnp.sin(turn)])
    local = jnp.arange(KEPT_Z, dtype=i32) - 1
    wanted = residue + SPANS * jnp.arange(ZS, dtype=i32)
    angle = (wanted[:, None] * local[None, :] % NZ).astype(f32) * (2.0 * math.pi / NZ)
    cosine, sine = jnp.cos(angle), jnp.sin(angle)
    phases = jnp.concatenate(
        [jnp.concatenate([cosine, sine], axis=1), jnp.concatenate([-sine, cosine], axis=1)], axis=0
    )
    return transform(turns, phases, pieces)


def solution(mesh):
    placed = (
        P(None, ("slab", "span")),
        P(None, ("slab", "span")),
        P(None, ("slab", "span")),
        P(("slab", "span"), None),
    )
    return jax.shard_map(
        shards,
        mesh=mesh,
        in_specs=placed,
        out_specs=P(None, None, "slab", "span", None),
        check_vma=False,
    )
```

```python
import functools
import math

import jax
import jax.numpy as jnp
import numpy as np
from jax import lax
from jax.experimental import pallas as pl
from jax.experimental.pallas import tpu as pltpu
from jax.sharding import PartitionSpec as P

CX = 2
NY = 128
NZ = 512
SLABS = 32
SPANS = 8
ZS = NZ // SPANS
COUNT = 16384
CAP = 1024
LANES = 128
GROUPS = COUNT // LANES
ROWS_Z = 80
KEPT_Z = 72
ROWS_X = CX + 3
STEP_GROUPS = 16
COLS = 256
bf16 = jnp.bfloat16
f32 = jnp.float32
i32 = jnp.int32

NT = (((1,), (1,)), ((), ()))


def one_hot_tile(row, rows_each, sublane):
    apart = 16 // rows_each
    row = jnp.broadcast_to(row, (16, LANES))
    met = (row & (apart - 1)) == sublane // rows_each
    return jnp.where(met, row >> (apart.bit_length() - 1), -1).astype(f32).astype(bf16)


def bucket_kernel(force_in, offset_in, cell_in, slab_in, out, force, offset, cell, slab, placed, wide, bases, firsts, stage, rows_0, rows_1, slots_0, slots_1, sems):
    copies = [
        pltpu.make_async_copy(source, target, sems.at[n])
        for n, (source, target) in enumerate(
            ((slab_in, slab), (force_in, force), (offset_in, offset), (cell_in, cell))
        )
    ]
    for copy in copies:
        copy.start()
    bucket = lax.broadcasted_iota(i32, (SLABS, LANES), 0)
    lane = lax.broadcasted_iota(i32, (SLABS, LANES), 1)
    row = lax.broadcasted_iota(i32, (LANES, 2 * LANES), 0)
    col = lax.broadcasted_iota(i32, (LANES, 2 * LANES), 1)
    before = jnp.where((col >= LANES) | (row < col), 1.0, 0.0).astype(bf16)
    sublane = lax.broadcasted_iota(i32, (16, LANES), 0)
    zero = jnp.zeros((16, LANES), bf16)
    one = jnp.ones((16, LANES), bf16)
    stage[...] = jnp.zeros_like(stage)
    copies[0].wait()

    def count(index, state):
        carry, starts, furthest = state
        chunk_first = carry & -LANES
        owners = slab[pl.ds(pl.multiple_of(index * 8, 8), 8), :]
        member = [bucket == owners[j : j + 1, :] for j in range(8)]
        stacked = jnp.concatenate([jnp.where(m, 1.0, 0.0).astype(bf16) for m in member], axis=0)
        counted = jnp.dot(stacked, before, preferred_element_type=f32)
        ranks, ahead = [], []
        for j in range(8):
            part = counted[SLABS * j : SLABS * (j + 1)]
            within = part[:, :LANES] + (carry & (LANES - 1)).astype(f32)
            ranks.append(jnp.sum(jnp.where(member[j], within, 0.0), axis=0, keepdims=True))
            within = part[:, :LANES] + (carry - chunk_first).astype(f32)
            ahead.append(jnp.sum(jnp.where(member[j], within, 0.0), axis=0, keepdims=True))
            starts = jnp.where(lane == index * 8 + j, carry >> 7, starts)
            carry = carry + part[:, LANES:].astype(i32)
        here = pl.ds(pl.multiple_of(index * 8, 8), 8)
        ahead = jnp.concatenate(ahead, axis=0)
        placed[here, :] = jnp.concatenate(ranks, axis=0).astype(i32)
        wide[here, :] = ahead.astype(i32)
        return carry, starts, jnp.maximum(furthest, ahead)

    none = jnp.zeros((SLABS, LANES), i32)
    _, starts, furthest = lax.fori_loop(
        0, GROUPS // 8, count, (none, none, jnp.zeros((8, LANES), f32)), unroll=4
    )
    windowed = jnp.max(furthest) < 2 * LANES - 0.5
    firsts[...] = starts
    last = pltpu.make_async_copy(firsts, bases, sems.at[4])
    last.start()
    for copy in copies[1:]:
        copy.wait()
    last.wait()

    def valued(g):
        here = pl.ds(pl.multiple_of(g * LANES, LANES), LANES)
        cells = cell[:, here]
        both = (cells[0:1, :] + 1) * ZS + cells[2:3, :]
        return jnp.concatenate(
            [force[:, here], offset[:, here], cells[1:2, :].astype(f32), both.astype(f32)], axis=0
        )

    def group(g):
        values = valued(g)
        values = jnp.concatenate([values, values], axis=0)
        upper = values.astype(bf16)
        lower = (values - upper.astype(f32)).astype(bf16)
        owner_tile = one_hot_tile(slab[pl.ds(g, 1), :], 8, sublane)
        place_tile = one_hot_tile(placed[pl.ds(g, 1), :], 1, sublane)
        rows, slots = [], []
        for t in range(16):
            hit = owner_tile == jnp.asarray(t, bf16)
            rows.append(jnp.concatenate([jnp.where(hit, upper, zero), jnp.where(hit, lower, zero)], axis=1))
            slot = jnp.where(place_tile == jnp.asarray(t, bf16), one, zero)
            slots.append(jnp.concatenate([slot, slot], axis=1))
        return lax.dot_general(
            jnp.concatenate(rows, axis=0), jnp.concatenate(slots, axis=0), NT, preferred_element_type=f32
        )

    def place(g, _):
        moved = group(g)
        for d in range(SLABS):
            first = bases[d, g]
            stage[d, first] += moved[8 * d : 8 * d + 8, :LANES]
            stage[d, first + 1] += moved[8 * d : 8 * d + 8, LANES:]
        return 0

    def build(chunk, rows, slots):
        for j in range(8):
            g = chunk * 8 + j
            lanes = slice(j * LANES, (j + 1) * LANES)
            values = valued(g)
            lower = values - values.astype(bf16).astype(f32)
            values = jnp.concatenate([values, lower], axis=0).astype(bf16)
            owner = jnp.broadcast_to(slab[pl.ds(g, 1), :], (16, LANES)).astype(f32).astype(bf16)
            place_tile = one_hot_tile(wide[pl.ds(g, 1), :], 1, sublane)
            for d in range(SLABS):
                rows[16 * d : 16 * d + 16, lanes] = jnp.where(owner == jnp.asarray(d, bf16), values, zero)
            for t in range(16):
                slots[16 * t : 16 * t + 16, lanes] = jnp.where(
                    place_tile == jnp.asarray(t, bf16), one, zero
                )

    def take(chunk, rows, slots):
        moved = lax.dot_general(rows[...], slots[...], NT, preferred_element_type=f32)
        for d in range(SLABS):
            first = bases[d, chunk * 8]
            both = moved[16 * d : 16 * d + 8] + moved[16 * d + 8 : 16 * d + 16]
            stage[d, first] += both[:, :LANES]
            stage[d, first + 1] += both[:, LANES:]

    @pl.when(windowed)
    def _():
        build(0, rows_0, slots_0)

        def step(index, _):
            build(2 * index + 1, rows_1, slots_1)
            take(2 * index, rows_0, slots_0)
            build(jnp.minimum(2 * index + 2, GROUPS // 8 - 1), rows_0, slots_0)
            take(2 * index + 1, rows_1, slots_1)
            return 0

        lax.fori_loop(0, GROUPS // 16, step, 0)

    @pl.when(jnp.logical_not(windowed))
    def _():
        lax.fori_loop(0, GROUPS, place, 0)

    def emit(d, _):
        is_last = lax.broadcasted_iota(i32, (8, LANES), 0) == 7
        spans_z = []
        for b in range(8):
            values = stage[d, b]
            both = values[7:8, :].astype(i32)
            out[d, b * 8 : b * 8 + 8, :] = jnp.where(
                is_last, jnp.broadcast_to((both >> 6).astype(f32), (8, LANES)), values
            )
            spans_z.append((both & (ZS - 1)).astype(f32))
        out[d, 64:72, :] = jnp.concatenate(spans_z, axis=0)
        return 0

    lax.fori_loop(0, SLABS, emit, 0, unroll=4)


def bucketed(force, offset, cell, slab):
    return pl.pallas_call(
        bucket_kernel,
        out_shape=jax.ShapeDtypeStruct((SLABS, 72, LANES), f32),
        in_specs=[pl.BlockSpec(memory_space=pl.ANY)] * 4,
        out_specs=pl.BlockSpec(memory_space=pltpu.VMEM),
        scratch_shapes=[
            pltpu.VMEM((3, COUNT), f32),
            pltpu.VMEM((3, COUNT), f32),
            pltpu.VMEM((3, COUNT), i32),
            pltpu.VMEM((GROUPS, LANES), i32),
            pltpu.VMEM((GROUPS, LANES), i32),
            pltpu.VMEM((GROUPS, LANES), i32),
            pltpu.SMEM((SLABS, LANES), i32),
            pltpu.VMEM((SLABS, LANES), i32),
            pltpu.VMEM((SLABS, 10, 8, LANES), f32),
            pltpu.VMEM((16 * SLABS, 8 * LANES), bf16),
            pltpu.VMEM((16 * SLABS, 8 * LANES), bf16),
            pltpu.VMEM((256, 8 * LANES), bf16),
            pltpu.VMEM((256, 8 * LANES), bf16),
            pltpu.SemaphoreType.DMA((5,)),
        ],
        compiler_params=pltpu.CompilerParams(vmem_limit_bytes=62 * 2**20),
        name="bucket_markers",
    )(force, offset, cell, slab)


SINE_TERMS = (
    0.39269908001633835,
    -0.1614909401096207,
    0.019922480650110423,
    -0.0011685376672223781,
    3.791877944380962e-05,
)


def quarter_sine(turn):
    square = turn * turn
    total = SINE_TERMS[-1]
    for term in SINE_TERMS[-2::-1]:
        total = term + square * total
    return turn * total


def quarter_pattern(above, sine, cosine):
    wave = jnp.where((above & 1) == 1, sine, cosine)
    return 0.25 + jnp.where(((above + 1) & 2) == 2, wave, -wave)


def spread_kernel(got, own, up, down, listed, rows_0, rows_1, cols_0, cols_1, total):
    total[...] = jnp.zeros_like(total)
    for cols in (cols_0, cols_1):
        cols[3 * ROWS_Z :, :] = jnp.zeros((COLS - 3 * ROWS_Z, STEP_GROUPS * LANES), bf16)
    row = lax.broadcasted_iota(i32, (8, LANES), 0)
    is_last = row == 7
    is_offset = (row >= 3) & (row < 6)

    def enlist(source, count):
        used = jnp.zeros((8, LANES), f32)
        for b in range(8):
            used = used + jnp.where(got[source, b * 8 : b * 8 + 8, :] > 0.5, 1.0, 0.0)
        filled = jnp.sum(jnp.where(is_last, used, 0.0)).astype(i32)
        for b in range(8):
            listed[count + b] = source * 8 + b
        return count + (filled + LANES - 1) // LANES

    count = lax.fori_loop(0, SLABS, enlist, jnp.int32(0), unroll=4)
    listed[count] = 0
    steps = (count + STEP_GROUPS - 1) // STEP_GROUPS
    sublane = lax.broadcasted_iota(i32, (16, LANES), 0)
    zero = jnp.zeros((16, LANES), bf16)

    def met_tile(above):
        above = above.astype(jnp.int16)
        return jnp.where((above & 15) < 4, above >> 4, jnp.int16(-1))

    def doubled(value):
        return jnp.concatenate([value, value], axis=0).astype(bf16)

    def spread_out(row):
        return jnp.broadcast_to(row, (8, LANES))

    def build(index, rows, cols):
        for j in range(STEP_GROUPS):
            position = index * STEP_GROUPS + j
            chosen = listed[jnp.minimum(position, count)]
            source, b = chosen >> 3, chosen & 7
            lanes = slice(j * LANES, (j + 1) * LANES)
            values = got[source, pl.ds(pl.multiple_of(b * 8, 8), 8), :]
            cell_z = got[source, pl.ds(64 + b, 1), :].astype(i32)
            cell_y = values[6:7].astype(i32)
            keep = jnp.where(position < count, 1.0, 0.0)
            turn = jnp.where(is_offset, values, 1.0 - pltpu.roll(values, 4, 0))
            wave = quarter_sine(turn)
            above_y = jnp.broadcast_to(cell_y + 2, (16, LANES)) - sublane
            above_z = jnp.broadcast_to(cell_z + 3, (16, LANES)) - sublane
            pattern_y = quarter_pattern(above_y[:8], spread_out(wave[4:5]), spread_out(wave[0:1]))
            pattern_z = keep * quarter_pattern(
                above_z[:8], spread_out(wave[5:6]), spread_out(wave[1:2])
            )
            sine_x, cosine_x = spread_out(wave[3:4]), spread_out(wave[7:8])
            weights = [0.25 - sine_x, 0.25 + cosine_x, 0.25 + sine_x, 0.25 - cosine_x]
            second = spread_out(values[7:8]) > 1.5
            planes = []
            for r in range(ROWS_X):
                at_zero = weights[r] if r < 4 else 0.0
                at_one = weights[r - 1] if r > 0 else 0.0
                planes.append(doubled(pattern_y * jnp.where(second, at_one, at_zero)))
            forces = [doubled(pattern_z * spread_out(values[c : c + 1])) for c in range(3)]
            met_y = met_tile(above_y)
            met_z = met_tile(above_z)
            for t in range(NY // 16):
                hit = met_y == jnp.int16(t)
                for x in range(ROWS_X):
                    start = x * NY + t * 16
                    rows[start : start + 16, lanes] = jnp.where(hit, planes[x], zero)
            for t in range(ROWS_Z // 16):
                hit = met_z == jnp.int16(t)
                for c in range(3):
                    start = c * ROWS_Z + t * 16
                    cols[start : start + 16, lanes] = jnp.where(hit, forces[c], zero)

    def take(rows, cols):
        total[...] += lax.dot_general(rows[...], cols[...], NT, preferred_element_type=f32)

    build(0, rows_0, cols_0)

    def step(index, _):
        build(2 * index + 1, rows_1, cols_1)
        take(rows_0, cols_0)
        build(2 * index + 2, rows_0, cols_0)
        take(rows_1, cols_1)
        return 0

    lax.fori_loop(0, (steps + 1) // 2, step, 0)

    for x in range(ROWS_X):
        plane = total[x * NY : (x + 1) * NY, :].T
        target = (down, own.at[0], own.at[1], up.at[0], up.at[1])[x]
        for c in range(3):
            target[c * KEPT_Z : (c + 1) * KEPT_Z, :] = plane[c * ROWS_Z : c * ROWS_Z + KEPT_Z, :]


def spread(got):
    block = jax.ShapeDtypeStruct((2, 3 * KEPT_Z, NY), f32)
    return pl.pallas_call(
        spread_kernel,
        out_shape=(block, block, jax.ShapeDtypeStruct((3 * KEPT_Z, NY), f32)),
        in_specs=[pl.BlockSpec(memory_space=pltpu.VMEM)],
        out_specs=(pl.BlockSpec(memory_space=pltpu.VMEM),) * 3,
        scratch_shapes=[
            pltpu.SMEM((SLABS * 8 + 8,), i32),
            pltpu.VMEM((ROWS_X * NY, STEP_GROUPS * LANES), bf16),
            pltpu.VMEM((ROWS_X * NY, STEP_GROUPS * LANES), bf16),
            pltpu.VMEM((COLS, STEP_GROUPS * LANES), bf16),
            pltpu.VMEM((COLS, STEP_GROUPS * LANES), bf16),
            pltpu.VMEM((ROWS_X * NY, COLS), f32),
        ],
        compiler_params=pltpu.CompilerParams(vmem_limit_bytes=40 * 2**20),
        name="spread_forces",
    )(got)


def fold_kernel(turns, *refs):
    out = refs[-1]
    for x in range(2):
        blocks = [piece[...] for piece in refs[x:-1:2]]
        for part in range(2):
            out[part, x] = sum(block * turns[part, n] for n, block in enumerate(blocks))


def fold(turns, pieces):
    return pl.pallas_call(
        fold_kernel,
        out_shape=jax.ShapeDtypeStruct((2, 2, 3 * KEPT_Z, NY), f32),
        in_specs=[pl.BlockSpec(memory_space=pltpu.SMEM)]
        + [pl.BlockSpec(memory_space=pltpu.VMEM)] * len(pieces),
        out_specs=pl.BlockSpec(memory_space=pltpu.VMEM),
        compiler_params=pltpu.CompilerParams(vmem_limit_bytes=40 * 2**20),
        cost_estimate=pl.CostEstimate(
            flops=4 * len(pieces) * 3 * KEPT_Z * NY,
            bytes_accessed=4 * (len(pieces) + 4) * 3 * KEPT_Z * NY,
            transcendentals=0,
        ),
        name="fold_arrived",
    )(turns, *pieces)


def transform_kernel(turns, phases, arrived, last_0, last_1, out):
    last = (last_0[...], last_1[...])
    real = [arrived[0, x] + last[x] * turns[0, SPANS - 1] for x in range(2)]
    imag = [arrived[1, x] + last[x] * turns[1, SPANS - 1] for x in range(2)]
    for c in range(3):
        rows = slice(c * KEPT_Z, (c + 1) * KEPT_Z)
        folded = jnp.concatenate(
            [jnp.concatenate([part[x][rows] for x in range(2)], axis=1) for part in (real, imag)],
            axis=0,
        )
        result = jnp.dot(
            phases[...], folded, precision=lax.Precision.HIGHEST, preferred_element_type=f32
        )
        for part in range(2):
            for x in range(2):
                out[part, c, x] = result[part * ZS : (part + 1) * ZS, x * NY : (x + 1) * NY]


def transform(turns, phases, pieces):
    return pl.pallas_call(
        transform_kernel,
        out_shape=jax.ShapeDtypeStruct((2, 3, CX, ZS, NY), f32),
        in_specs=[pl.BlockSpec(memory_space=pltpu.SMEM)]
        + [pl.BlockSpec(memory_space=pltpu.VMEM)] * (1 + len(pieces)),
        out_specs=pl.BlockSpec(memory_space=pltpu.VMEM),
        compiler_params=pltpu.CompilerParams(vmem_limit_bytes=40 * 2**20),
        name="fold_and_transform",
    )(turns, phases, *pieces)


def shards(marker_force, marker_offset, marker_cell, marker_slab):
    sent = bucketed(
        marker_force, marker_offset, marker_cell, marker_slab.reshape(GROUPS, LANES)
    )
    got = lax.all_to_all(sent, "slab", split_axis=0, concat_axis=0, tiled=True)
    own, up, down = spread(got)
    upward = [(i, i + 1) for i in range(SLABS - 1)]
    from_below = lax.ppermute(up, "slab", upward)
    from_above = lax.ppermute(down, "slab", [(j, i) for i, j in upward])
    field = own + from_below
    field = jnp.stack([field[0], field[1] + from_above])

    span = lax.axis_index("span")
    residue = ((span & 1) << 2) | (span & 2) | (span >> 2)
    forward = [(i, (i + 1) % SPANS) for i in range(SPANS)]
    backward = [(j, i) for i, j in forward]
    pieces, apart = [field[0], field[1]], [0]
    ahead, behind = [field[0], field[1]], [field[0], field[1]]
    for hop in range(1, SPANS // 2):
        ahead[0] = lax.ppermute(ahead[0], "span", forward)
        behind[1] = lax.ppermute(behind[1], "span", backward)
        ahead[1] = lax.ppermute(ahead[1], "span", forward)
        behind[0] = lax.ppermute(behind[0], "span", backward)
        pieces += ahead + behind
        apart += [-hop, hop]
    pieces.append(lax.ppermute(ahead[0], "span", forward))
    pieces.append(lax.ppermute(behind[1], "span", backward))
    apart.append(SPANS // 2)
    origin = (span + jnp.asarray(apart, i32)) % SPANS
    turn = (residue * origin % SPANS).astype(f32) * (2.0 * math.pi / SPANS)
    turns = jnp.stack([jnp.cos(turn), -jnp.sin(turn)])
    local = jnp.arange(KEPT_Z, dtype=i32) - 1
    wanted = residue + SPANS * jnp.arange(ZS, dtype=i32)
    angle = (wanted[:, None] * local[None, :] % NZ).astype(f32) * (2.0 * math.pi / NZ)
    cosine, sine = jnp.cos(angle), jnp.sin(angle)
    phases = jnp.concatenate(
        [jnp.concatenate([cosine, sine], axis=1), jnp.concatenate([-sine, cosine], axis=1)], axis=0
    )
    arrived = fold(turns, pieces[:-2])
    return transform(turns, phases, [arrived] + pieces[-2:])


def solution(mesh):
    placed = (
        P(None, ("slab", "span")),
        P(None, ("slab", "span")),
        P(None, ("slab", "span")),
        P(("slab", "span"), None),
    )
    return jax.shard_map(
        shards,
        mesh=mesh,
        in_specs=placed,
        out_specs=P(None, None, "slab", "span", None),
        check_vma=False,
    )
```
